32 devices in a mesh: band: 2 (over x), blk: 16 (over z, y, core).
Axes of the slice: x: 2, y: 2, z: 4, core: 2. Of those that a mesh axis runs over, the one named last changes fastest.
Arguments:
- amps: bfloat16 [2560, 16, 128], P(None, 'blk'), may hold values from -6 to 6
- beam: float32 [2, 2560], P('band'), may hold values from 0.2 to 1
- legendre: bfloat16 [16, 2560, 64], P('blk'), as said below
- m_values: int32 [16], replicated, may hold values from 0 to 2559, as said below
- cycle_order: int32 [64], replicated, may hold values from 0 to 63, each once
- pixel_counts: int32 [64], replicated, may hold values from 512 to 4096, as said below
- inv_noise: float32 [2, 64, 4096], P('band', 'blk'), may hold values from 0.1 to 2
Outputs:
- amps_out: float32 [2560, 16, 128], P('band', 'blk')
The draws below stay inside these ranges and needn't reach their ends.
Inputs may be any that keep to these rules, and one draw needn't show every extreme that they name: `m_values`: distinct orders; both 0 and 2559 occur. legendre[m, l, s] is zero wherever l < m_values[m]. `pixel_counts`: some cycle has exactly 4096 pixels.
All inputs are finite; a program needn't handle non-finite values.
Results may differ from the reference program's by a relative error of at most 0.0017.
Values may be sent and summed in bfloat16 or wider, within the bound.
No kernel may reach another device: no remote copies, remote signals or barrier semaphores. Data moves between devices by JAX's collectives and lax.ppermute only.
A program may use at most 64 MiB of HBM per device.

```python
import math
import jax
import jax.numpy as jnp
from jax import lax

DEGREES = 2560
PIX = 4096
CHAINS = 64
BANDS = 2
ORDERS = 16
CYCLES = 64


def drawn_orders(key):
    base_key = jax.random.fold_in(key, 11)
    inner = 1 + jax.random.permutation(jax.random.fold_in(base_key, 1), DEGREES - 2)[:ORDERS - 2]
    chosen = jnp.concatenate([jnp.array([0, DEGREES - 1], jnp.int32), inner.astype(jnp.int32)])
    return jax.random.permutation(jax.random.fold_in(base_key, 2), chosen).astype(jnp.int32)


def draw_m_values(key, part):
    return drawn_orders(key)


def draw_legendre(key, part):
    orders_now = drawn_orders(key)
    values = jax.random.normal(jax.random.fold_in(key, 12), (ORDERS, DEGREES, CYCLES), jnp.float32)
    values = values * jnp.float32((DEGREES * CYCLES) ** (-0.25))
    degree_idx = jnp.arange(DEGREES, dtype=jnp.int32)
    keep = degree_idx[None, :, None] >= orders_now[:, None, None]
    return jnp.where(keep, values, jnp.float32(0.0)).astype(jnp.bfloat16)


def draw_pixel_counts(key, part):
    counts_drawn = jax.random.randint(jax.random.fold_in(key, 13), (CYCLES,), PIX // 8, PIX + 1).astype(jnp.int32)
    position = jax.random.randint(jax.random.fold_in(key, 14), (), 0, CYCLES)
    return counts_drawn.at[position].set(PIX).astype(jnp.int32)


def shard_levels(stream_key, shape, pieces, smallest, high):
    level = 1.0
    for dim, blocks in pieces:
        steps = jax.random.uniform(jax.random.fold_in(jax.random.fold_in(stream_key, 6), dim), (blocks,), jnp.float32, smallest / len(pieces), high / len(pieces))
        level = level * jnp.repeat(jnp.exp(steps), shape[dim] // blocks).reshape((-1,) + (1,) * (len(shape) - 1 - dim))
    return level


def bell_draw(own_key, shape, spread, most, cuts=(), held_as=jnp.bfloat16):
    loudness = shard_levels(own_key, shape, cuts, -0.22, 0.18) if cuts else 1.0
    entries = jax.random.normal(own_key, shape, jnp.float32) * spread * loudness
    return jnp.minimum(jnp.maximum(entries, -most), most).astype(held_as)


def setup_inputs(seed: int = 0) -> dict:
    key_list = jax.random.split(jax.random.key(seed), 8)
    return {
        "amps": bell_draw(key_list[0], (DEGREES, ORDERS, 2 * CHAINS), 1.0, 6.0, ((1, 16),)),
        "beam": jnp.clip(jnp.exp(math.log(1.0) - 1.609438 * jax.random.uniform(key_list[1], (BANDS, DEGREES), jnp.float32) ** shard_levels(key_list[1], (BANDS, DEGREES), ((0, 2),), -0.2, 0.2)), 0.2, 1.0),
        "legendre": draw_legendre(jax.random.fold_in(key_list[7], 71), 0),
        "m_values": draw_m_values(jax.random.fold_in(key_list[7], 71), 0),
        "cycle_order": jax.random.permutation(key_list[4], CYCLES).astype(jnp.int32),
        "pixel_counts": draw_pixel_counts(jax.random.fold_in(key_list[7], 71), 0),
        "inv_noise": jnp.clip(jnp.exp(math.log(2.0) - 2.9957323 * jax.random.uniform(key_list[6], (BANDS, CYCLES, PIX), jnp.float32) ** shard_levels(key_list[6], (BANDS, CYCLES, PIX), ((0, 2), (1, 16)), -0.2, 0.2)), 0.1, 2.0),
    }


def cycle_table(order_ids, cycle_id, pixel_count, pixels):
    pixel_idx = jnp.arange(pixels, dtype=jnp.int32)
    product_mod = order_ids[:, None] * pixel_idx[None, :] % pixel_count
    parity = cycle_id % 2
    numerator = (2 * product_mod + order_ids[:, None] * parity) % (2 * pixel_count)
    phase_angle = numerator.astype(jnp.float32) * (jnp.float32(math.pi) / pixel_count.astype(jnp.float32))
    inside = (pixel_idx < pixel_count)[None, :]
    norm_scale = lax.rsqrt(pixel_count.astype(jnp.float32))
    cos_part = jnp.where(inside, jnp.cos(phase_angle) * norm_scale, jnp.float32(0.0))
    sin_part = jnp.where(inside, -jnp.sin(phase_angle) * norm_scale, jnp.float32(0.0))
    return jnp.stack([cos_part, sin_part], axis=1).reshape(2 * order_ids.shape[0], pixels)

def cycle_pass(modes_in, phase_table, weights):
    orders = modes_in.shape[0]
    chains = modes_in.shape[1] // 2
    modes_flat = modes_in.reshape(2 * orders, chains)
    pixel_field = lax.dot_general(modes_flat, phase_table, (((0,), (0,)), ((), ())), precision=lax.Precision.HIGHEST)
    weighted_field = pixel_field * weights[None, :]
    projected = lax.dot_general(phase_table, weighted_field, (((1,), (1,)), ((), ())), precision=lax.Precision.HIGHEST)
    return projected.reshape(orders, 2 * chains)

def reference(amps, beam, legendre, m_values, cycle_order, pixel_counts, inv_noise):
    accum = jnp.zeros(amps.shape, jnp.float32)
    amps_major = jnp.swapaxes(amps, 0, 1)
    for band_idx in range(BANDS):
        gains = beam[band_idx]
        weighted = (amps_major.astype(jnp.float32) * gains[None, :, None]).astype(jnp.bfloat16)

        def synth_one(packed):
            return lax.dot_general(packed[0], packed[1], (((0,), (0,)), ((), ())), preferred_element_type=jnp.float32)
        synth = lax.map(synth_one, (legendre, weighted))
        cycle_major = jnp.swapaxes(synth, 0, 1)
        cycle_counts = pixel_counts[cycle_order]

        def cycle_one(packed):
            phase_table = cycle_table(m_values, packed[1], packed[2], PIX)
            return cycle_pass(packed[0], phase_table, packed[3])
        projected = lax.map(cycle_one, (cycle_major, cycle_order, cycle_counts, inv_noise[band_idx]))
        proj_half = jnp.swapaxes(projected.astype(jnp.bfloat16), 0, 1)

        def analyse_one(packed):
            return jnp.dot(packed[0], packed[1], preferred_element_type=jnp.float32)
        analysed = lax.map(analyse_one, (legendre, proj_half))
        accum = accum + jnp.swapaxes(analysed, 0, 1) * gains[:, None, None]
    return accum
```

```python
import functools
import math

import jax
import jax.numpy as jnp
from jax import lax
from jax.experimental import pallas as pl
from jax.experimental.pallas import tpu as pltpu
from jax.sharding import PartitionSpec as P

LANES = 128
VMEM = pltpu.CompilerParams(vmem_limit_bytes=48 * 1024 * 1024)
NT = (((1,), (1,)), ((), ()))


def synth_kernel(amps_ref, beam_ref, leg_ref, out_ref, weighted):
    chunks = beam_ref.shape[0]
    gains = beam_ref[...].T
    for k in range(chunks):
        rows = pl.ds(k * LANES, LANES)
        product = amps_ref[rows, :].astype(jnp.float32) * gains[:, k : k + 1]
        weighted[rows, :] = product.astype(jnp.bfloat16)
    out_ref[...] = jnp.dot(leg_ref[...], weighted[...], preferred_element_type=jnp.float32)


def mod_exact(value, modulus):
    quotient = (value.astype(jnp.float32) / modulus.astype(jnp.float32)).astype(jnp.int32)
    left = value - quotient * modulus
    left = jnp.where(left < 0, left + modulus, left)
    return jnp.where(left >= modulus, left - modulus, left)


def cos_sin(numer, count):
    countf = count.astype(jnp.float32)
    quarter = ((2 * numer + (count >> 1)).astype(jnp.float32) / countf).astype(jnp.int32)
    rest = (2 * numer - quarter * count).astype(jnp.float32)
    angle = rest * (jnp.float32(math.pi / 2) / countf)
    square = angle * angle
    sin = angle * (
        1.0 + square * (-1.0 / 6 + square * (1.0 / 120 + square * (-1.0 / 5040 + square * (1.0 / 362880))))
    )
    cos = 1.0 + square * (
        -0.5 + square * (1.0 / 24 + square * (-1.0 / 720 + square * (1.0 / 40320 - square * (1.0 / 3628800))))
    )
    odd = (quarter & 1) == 1
    cos_out = jnp.where(odd, sin, cos)
    sin_out = jnp.where(odd, cos, sin)
    cos_out = jnp.where(((quarter + 1) & 2) == 2, -cos_out, cos_out)
    sin_out = jnp.where((quarter & 2) == 2, -sin_out, sin_out)
    return cos_out, sin_out


def gram_kernel(start_ref, order_ref, cycle_ref, count_ref, noise_ref, gram_ref, high, low):
    cycles, pixels = noise_ref.shape
    orders = order_ref.shape[0]
    rows = orders * cycles
    start = start_ref[0]
    row = lax.broadcasted_iota(jnp.int32, (rows, LANES), 0)
    lane = lax.broadcasted_iota(jnp.int32, (rows, LANES), 1)
    slot = row % cycles
    count = jnp.zeros((rows, LANES), jnp.int32)
    parity = jnp.zeros((rows, LANES), jnp.int32)
    for i in range(cycles):
        cycle = cycle_ref[start + i]
        count = jnp.where(slot == i, count_ref[cycle], count)
        parity = jnp.where(slot == i, cycle & 1, parity)
    order = jnp.zeros((rows, LANES), jnp.int32)
    for m in range(orders):
        order = jnp.where(row // cycles == m, order_ref[m], order)
    fine_c, fine_s = cos_sin(mod_exact(2 * order * lane, 2 * count), count)
    coarse = 2 * LANES * order * (lane & (pixels // LANES - 1)) + order * parity
    coarse_c, coarse_s = cos_sin(mod_exact(coarse, 2 * count), count)
    norm = lax.rsqrt(count.astype(jnp.float32))
    fine_c, fine_s = fine_c * norm, fine_s * norm
    coarse_s = -coarse_s

    pixel = lax.broadcasted_iota(jnp.int32, (cycles, pixels), 1)
    inside = pixel < count[:cycles, :1]
    root = jnp.sqrt(jnp.where(inside, noise_ref[...], 0.0))
    reps = max(8 // cycles, 1)
    root = jnp.concatenate([root] * reps, axis=0)
    period = root.shape[0]

    step = 2
    total = jnp.zeros((2 * rows, 4 * rows), jnp.float32)
    for block in range(pixels // LANES // step):
        for j in range(block * step, (block + 1) * step):
            cols = slice(j * LANES, (j + 1) * LANES)
            here = jnp.concatenate([root[:, cols]] * (rows // period), axis=0)
            a_c, a_s = coarse_c[:, j : j + 1], coarse_s[:, j : j + 1]
            for c, value in enumerate((a_c * fine_c + a_s * fine_s, a_s * fine_c - a_c * fine_s)):
                value = value * here
                top = value.astype(jnp.bfloat16)
                high[c * rows : (c + 1) * rows, cols] = top
                low[c * rows : (c + 1) * rows, cols] = (value - top.astype(jnp.float32)).astype(jnp.bfloat16)
        cols = slice(block * step * LANES, (block + 1) * step * LANES)
        top = high[:, cols]
        both = jnp.concatenate([top, low[:, cols]], axis=0)
        total = total + lax.dot_general(top, both, NT, preferred_element_type=jnp.float32)
    cross = total[:, 2 * rows :]
    gram = total[:, : 2 * rows] + cross + cross.T
    row = lax.broadcasted_iota(jnp.int32, gram.shape, 0)
    col = lax.broadcasted_iota(jnp.int32, gram.shape, 1)
    gram_ref[...] = jnp.where(row % cycles == col % cycles, gram, 0.0)


def apply_kernel(bands, gram_ref, modes_ref, out_ref):
    rows, width = modes_ref.shape
    chains = width // 2
    modes = modes_ref[...]
    stacked = jnp.concatenate([modes[:, :chains], modes[:, chains:]], axis=0)
    result = jnp.dot(
        gram_ref[...], stacked, precision=lax.Precision.HIGHEST, preferred_element_type=jnp.float32
    )
    half = jnp.concatenate([result[:rows], result[rows:]], axis=1).astype(jnp.bfloat16)
    for b in range(bands):
        out_ref[b * rows : (b + 1) * rows, :] = half


def analysis_kernel(bands, gain_ref, leg_ref, half_ref, out_ref):
    cycles, degrees = leg_ref.shape
    width = half_ref.shape[1]
    halves = [half_ref[b * cycles : (b + 1) * cycles, :] for b in range(bands)]
    right = jnp.concatenate(halves, axis=1)
    gains = gain_ref[...].T
    size = 256 if degrees % 256 == 0 else degrees
    for at in range(0, degrees, size):
        product = lax.dot_general(
            leg_ref[:, at : at + size],
            right,
            (((0,), (0,)), ((), ())),
            preferred_element_type=jnp.float32,
        )
        total = gains[at : at + size, 0:1] * product[:, :width]
        for b in range(1, bands):
            total = total + gains[at : at + size, b : b + 1] * product[:, b * width : (b + 1) * width]
        out_ref[at : at + size, :] = total


def shards(bands, amps, beam, legendre, m_values, cycle_order, pixel_counts, inv_noise):
    degrees, _, width = amps.shape
    cycles = legendre.shape[2]
    cycles_here = inv_noise.shape[1]
    orders = m_values.shape[0]
    rows = orders * cycles_here
    part = degrees // bands
    leg = jnp.swapaxes(legendre[0], 0, 1)
    smem = pl.BlockSpec(memory_space=pltpu.SMEM)
    vmem = pl.BlockSpec(memory_space=pltpu.VMEM)

    synth = pl.pallas_call(
        synth_kernel,
        out_shape=jax.ShapeDtypeStruct((cycles, width), jnp.float32),
        in_specs=[vmem] * 3,
        out_specs=vmem,
        scratch_shapes=[pltpu.VMEM((degrees, width), jnp.bfloat16)],
        compiler_params=VMEM,
    )(amps[:, 0, :], beam.reshape(degrees // LANES, LANES), leg)
    modes = lax.all_to_all(synth, "blk", split_axis=0, concat_axis=0, tiled=True)

    start = (lax.axis_index("blk") * cycles_here).astype(jnp.int32).reshape(1)
    gram = pl.pallas_call(
        gram_kernel,
        out_shape=jax.ShapeDtypeStruct((2 * rows, 2 * rows), jnp.float32),
        in_specs=[smem] * 4 + [vmem],
        out_specs=vmem,
        scratch_shapes=[pltpu.VMEM((2 * rows, inv_noise.shape[2]), jnp.bfloat16)] * 2,
        compiler_params=VMEM,
    )(start, m_values, cycle_order, pixel_counts, inv_noise[0])

    half = pl.pallas_call(
        functools.partial(apply_kernel, bands),
        out_shape=jax.ShapeDtypeStruct((bands * rows, width), jnp.bfloat16),
        in_specs=[vmem] * 2,
        out_specs=vmem,
        compiler_params=VMEM,
    )(gram, modes)
    half = lax.all_to_all(half, ("band", "blk"), split_axis=0, concat_axis=0, tiled=True)

    gains = lax.all_to_all(beam.reshape(bands, part), "band", split_axis=0, concat_axis=0, tiled=True)
    leg_part = lax.dynamic_slice_in_dim(leg, lax.axis_index("band") * part, part, axis=1)
    out = pl.pallas_call(
        functools.partial(analysis_kernel, bands),
        out_shape=jax.ShapeDtypeStruct((part, width), jnp.float32),
        in_specs=[vmem] * 3,
        out_specs=vmem,
        compiler_params=VMEM,
    )(gains, leg_part, half)
    return out[:, None, :]


def solution(mesh):
    return jax.shard_map(
        functools.partial(shards, mesh.shape["band"]),
        mesh=mesh,
        in_specs=(
            P(None, "blk", None),
            P("band", None),
            P("blk", None, None),
            P(),
            P(),
            P(),
            P("band", "blk", None),
        ),
        out_specs=P("band", "blk", None),
        check_vma=False,
    )
```

```python
import functools
import math

import jax
import jax.numpy as jnp
from jax import lax
from jax.experimental import pallas as pl
from jax.experimental.pallas import tpu as pltpu
from jax.sharding import PartitionSpec as P

LANES = 128
SLAB = 512
VMEM = pltpu.CompilerParams(vmem_limit_bytes=48 * 1024 * 1024)
NT = (((1,), (1,)), ((), ()))


def synth_kernel(bands, amps_hbm, beam_hbm, leg_hbm, out_ref, own_ref, amps, beam, leg, weighted, padded, sems):
    degrees = amps.shape[0]
    chunks = amps_hbm.shape[0] // SLAB
    cycles = leg.shape[0]
    band, blk = lax.axis_index("band"), lax.axis_index("blk")
    copies = [pltpu.make_async_copy(beam_hbm, beam, sems.at[0])]
    for k in range(chunks):
        at = pl.ds(k * SLAB, SLAB)
        copies.append(pltpu.make_async_copy(amps_hbm.at[at, :], amps.at[at, :], sems.at[1 + 2 * k]))
        copies.append(pltpu.make_async_copy(leg_hbm.at[:, at], leg.at[:, at], sems.at[2 + 2 * k]))
    for copy in copies:
        copy.start()
    copies[0].wait()
    gains = jnp.concatenate(
        [beam[0:1, k * LANES : (k + 1) * LANES] for k in range(degrees // LANES)], axis=0
    ).T
    part = degrees // bands
    lines = -(-part // LANES)
    padded[...] = jnp.zeros_like(padded)
    for p in range(bands):
        for t in range(lines):
            size = min(LANES, part - t * LANES)
            first = p * part + t * LANES
            padded[p * lines + t : p * lines + t + 1, :size] = beam[0:1, first : first + size]
    rows = cycles // lax.axis_size("blk")
    for p in range(bands):
        piece = padded[pl.ds(p * lines + blk * rows, rows), :]
        out_ref[p * cycles : (p + 1) * cycles, :] = jnp.concatenate([piece] * (cycles // rows), axis=0)
    own_ref[...] = padded[pl.ds(band * lines, lines), :]
    total = None
    for k in range(chunks):
        copies[1 + 2 * k].wait()
        copies[2 + 2 * k].wait()
        for j in range(k * SLAB, (k + 1) * SLAB, LANES):
            product = amps[j : j + LANES, :].astype(jnp.float32) * gains[:, j // LANES : j // LANES + 1]
            weighted[j : j + LANES, :] = product.astype(jnp.bfloat16)
        at = slice(k * SLAB, (k + 1) * SLAB)
        add = jnp.dot(leg[:, at], weighted[at, :], preferred_element_type=jnp.float32)
        total = add if total is None else total + add
    out_ref[pl.ds(pl.multiple_of(band * cycles, 8), cycles), :] = total


def mod_exact(value, modulus):
    quotient = (value.astype(jnp.float32) / modulus.astype(jnp.float32)).astype(jnp.int32)
    left = value - quotient * modulus
    left = jnp.where(left < 0, left + modulus, left)
    return jnp.where(left >= modulus, left - modulus, left)


def cos_sin(numer, count):
    countf = count.astype(jnp.float32)
    quarter = ((2 * numer + (count >> 1)).astype(jnp.float32) / countf).astype(jnp.int32)
    rest = (2 * numer - quarter * count).astype(jnp.float32)
    angle = rest * (jnp.float32(math.pi / 2) / countf)
    square = angle * angle
    sin = angle * (
        1.0 + square * (-1.0 / 6 + square * (1.0 / 120 + square * (-1.0 / 5040 + square * (1.0 / 362880))))
    )
    cos = 1.0 + square * (
        -0.5 + square * (1.0 / 24 + square * (-1.0 / 720 + square * (1.0 / 40320 - square * (1.0 / 3628800))))
    )
    odd = (quarter & 1) == 1
    cos_out = jnp.where(odd, sin, cos)
    sin_out = jnp.where(odd, cos, sin)
    cos_out = jnp.where(((quarter + 1) & 2) == 2, -cos_out, cos_out)
    sin_out = jnp.where((quarter & 2) == 2, -sin_out, sin_out)
    return cos_out, sin_out


def gram_kernel(start_ref, order_ref, cycle_ref, count_ref, noise_ref, gram_ref, high, low):
    cycles, pixels = noise_ref.shape
    orders = order_ref.shape[0]
    rows = orders * cycles
    start = start_ref[0]
    row = lax.broadcasted_iota(jnp.int32, (rows, LANES), 0)
    lane = lax.broadcasted_iota(jnp.int32, (rows, LANES), 1)
    slot = row % cycles
    count = jnp.zeros((rows, LANES), jnp.int32)
    parity = jnp.zeros((rows, LANES), jnp.int32)
    for i in range(cycles):
        cycle = cycle_ref[start + i]
        count = jnp.where(slot == i, count_ref[cycle], count)
        parity = jnp.where(slot == i, cycle & 1, parity)
    order = jnp.zeros((rows, LANES), jnp.int32)
    for m in range(orders):
        order = jnp.where(row // cycles == m, order_ref[m], order)
    fine_c, fine_s = cos_sin(mod_exact(2 * order * lane, 2 * count), count)
    coarse = 2 * LANES * order * (lane & (pixels // LANES - 1)) + order * parity
    coarse_c, coarse_s = cos_sin(mod_exact(coarse, 2 * count), count)
    norm = lax.rsqrt(count.astype(jnp.float32))
    fine_c, fine_s = fine_c * norm, fine_s * norm
    coarse_s = -coarse_s

    pixel = lax.broadcasted_iota(jnp.int32, (cycles, pixels), 1)
    inside = pixel < count[:cycles, :1]
    root = jnp.sqrt(jnp.where(inside, noise_ref[...], 0.0))
    reps = max(8 // cycles, 1)
    root = jnp.concatenate([root] * reps, axis=0)
    period = root.shape[0]

    step = 2
    total = jnp.zeros((2 * rows, 4 * rows), jnp.float32)
    for block in range(pixels // LANES // step):
        for j in range(block * step, (block + 1) * step):
            cols = slice(j * LANES, (j + 1) * LANES)
            here = jnp.concatenate([root[:, cols]] * (rows // period), axis=0)
            a_c, a_s = coarse_c[:, j : j + 1], coarse_s[:, j : j + 1]
            for c, value in enumerate((a_c * fine_c + a_s * fine_s, a_s * fine_c - a_c * fine_s)):
                value = value * here
                top = value.astype(jnp.bfloat16)
                high[c * rows : (c + 1) * rows, cols] = top
                low[c * rows : (c + 1) * rows, cols] = (value - top.astype(jnp.float32)).astype(jnp.bfloat16)
        cols = slice(block * step * LANES, (block + 1) * step * LANES)
        top = high[:, cols]
        both = jnp.concatenate([top, low[:, cols]], axis=0)
        total = total + lax.dot_general(top, both, NT, preferred_element_type=jnp.float32)
    cross = total[:, 2 * rows :]
    gram = total[:, : 2 * rows] + cross + cross.T
    row = lax.broadcasted_iota(jnp.int32, gram.shape, 0)
    col = lax.broadcasted_iota(jnp.int32, gram.shape, 1)
    gram = jnp.where(row % cycles == col % cycles, gram, 0.0)
    top = gram.astype(jnp.bfloat16)
    rest = (gram - top.astype(jnp.float32)).astype(jnp.bfloat16)
    gram_ref[...] = jnp.concatenate([top, top, rest], axis=1)


def apply_kernel(bands, gram_ref, modes_ref, out_ref):
    rows = gram_ref.shape[0] // 2
    width = modes_ref.shape[1]
    chains = width // 2
    cycles = modes_ref.shape[0] // bands
    modes = modes_ref[pl.ds(pl.multiple_of(lax.axis_index("band") * cycles, 8), cycles), :]
    stacked = jnp.concatenate([modes[:, :chains], modes[:, chains:]], axis=0)
    top = stacked.astype(jnp.bfloat16)
    rest = (stacked - top.astype(jnp.float32)).astype(jnp.bfloat16)
    right = jnp.concatenate([top, rest, top], axis=0)
    result = jnp.dot(gram_ref[...], right, preferred_element_type=jnp.float32)
    half = jnp.concatenate([result[:rows], result[rows:]], axis=1).astype(jnp.bfloat16)
    for b in range(bands):
        out_ref[b * rows : (b + 1) * rows, :] = half


def matrix_kernel(bands, modes_ref, own_ref, leg_ref, out_ref):
    cycles, part = leg_ref.shape
    lines = own_ref.shape[0]
    band = lax.axis_index("band")
    columns = []
    for b in range(bands):
        sent = modes_ref[b * cycles : b * cycles + lines, :]
        columns.append(jnp.where(band == b, own_ref[...], sent).T)
    for t in range(lines):
        size = min(LANES, part - t * LANES)
        turned = leg_ref[:, t * LANES : t * LANES + size].astype(jnp.float32).T
        scaled = [turned * column[:size, t : t + 1] for column in columns]
        scaled = jnp.concatenate(scaled, axis=1)
        top = scaled.astype(jnp.bfloat16)
        rest = (scaled - top.astype(jnp.float32)).astype(jnp.bfloat16)
        out_ref[t * LANES : t * LANES + size, :] = jnp.concatenate([top, rest], axis=1)


def analysis_kernel(matrix_ref, half_ref, out_hbm, out, sems):
    degrees = out.shape[0]
    size = 256 if degrees % 256 == 0 else degrees
    right = jnp.concatenate([half_ref[...]] * 2, axis=0)
    copies = []
    for k in range(degrees // size):
        at = pl.ds(k * size, size)
        out[at, :] = jnp.dot(matrix_ref[at, :], right, preferred_element_type=jnp.float32)
        copies.append(pltpu.make_async_copy(out.at[at, :], out_hbm.at[at, :], sems.at[k]))
        copies[-1].start()
    for copy in copies:
        copy.wait()


def shards(bands, amps, beam, legendre, m_values, cycle_order, pixel_counts, inv_noise):
    degrees, _, width = amps.shape
    cycles = legendre.shape[2]
    cycles_here = inv_noise.shape[1]
    orders = m_values.shape[0]
    rows = orders * cycles_here
    part = degrees // bands
    leg = jnp.swapaxes(legendre[0], 0, 1)
    smem = pl.BlockSpec(memory_space=pltpu.SMEM)
    vmem = pl.BlockSpec(memory_space=pltpu.VMEM)

    hbm = pl.BlockSpec(memory_space=pltpu.HBM)
    lines = -(-part // LANES)
    slabs = degrees // SLAB
    sent, own = pl.pallas_call(
        functools.partial(synth_kernel, bands),
        out_shape=[
            jax.ShapeDtypeStruct((bands * cycles, width), jnp.float32),
            jax.ShapeDtypeStruct((lines, LANES), jnp.float32),
        ],
        in_specs=[hbm] * 3,
        out_specs=[vmem] * 2,
        scratch_shapes=[
            pltpu.VMEM((degrees, width), jnp.bfloat16),
            pltpu.VMEM((1, degrees), jnp.float32),
            pltpu.VMEM((cycles, degrees), jnp.bfloat16),
            pltpu.VMEM((degrees, width), jnp.bfloat16),
            pltpu.VMEM((bands * lines + cycles, LANES), jnp.float32),
            pltpu.SemaphoreType.DMA((1 + 2 * slabs,)),
        ],
        compiler_params=pltpu.CompilerParams(vmem_limit_bytes=127 * 512 * 1024),
        cost_estimate=pl.CostEstimate(
            flops=2 * degrees * cycles * width, transcendentals=0, bytes_accessed=2 * degrees * (cycles + width)
        ),
    )(amps[:, 0, :], beam, leg)
    modes = lax.all_to_all(sent, ("band", "blk"), split_axis=0, concat_axis=0, tiled=True)

    start = (lax.axis_index("blk") * cycles_here).astype(jnp.int32).reshape(1)
    pixels = inv_noise.shape[2]
    gram = pl.pallas_call(
        gram_kernel,
        out_shape=jax.ShapeDtypeStruct((2 * rows, 6 * rows), jnp.bfloat16),
        in_specs=[smem] * 4 + [vmem],
        out_specs=vmem,
        scratch_shapes=[pltpu.VMEM((2 * rows, pixels), jnp.bfloat16)] * 2,
        compiler_params=VMEM,
        cost_estimate=pl.CostEstimate(
            flops=16 * rows * rows * pixels, transcendentals=0, bytes_accessed=8 * rows * pixels
        ),
    )(start, m_values, cycle_order, pixel_counts, inv_noise[0])

    half = pl.pallas_call(
        functools.partial(apply_kernel, bands),
        out_shape=jax.ShapeDtypeStruct((bands * rows, width), jnp.bfloat16),
        in_specs=[vmem] * 2,
        out_specs=vmem,
        compiler_params=VMEM,
    )(gram, modes)
    half, modes, own, leg = lax.optimization_barrier((half, modes, own, leg))
    half = lax.all_to_all(half, ("band", "blk"), split_axis=0, concat_axis=0, tiled=True)

    leg_part = lax.dynamic_slice_in_dim(leg, lax.axis_index("band") * part, part, axis=1)
    matrix = pl.pallas_call(
        functools.partial(matrix_kernel, bands),
        out_shape=jax.ShapeDtypeStruct((part, 2 * bands * cycles), jnp.bfloat16),
        in_specs=[vmem] * 3,
        out_specs=vmem,
        compiler_params=VMEM,
        cost_estimate=pl.CostEstimate(
            flops=8 * part * bands * cycles, transcendentals=0, bytes_accessed=4 * part * bands * cycles
        ),
    )(modes, own, leg_part)
    out = pl.pallas_call(
        analysis_kernel,
        out_shape=jax.ShapeDtypeStruct((part, width), jnp.float32),
        in_specs=[vmem] * 2,
        out_specs=hbm,
        scratch_shapes=[pltpu.VMEM((part, width), jnp.float32), pltpu.SemaphoreType.DMA((max(part // 256, 1),))],
        compiler_params=VMEM,
    )(matrix, half)
    return out[:, None, :]


def solution(mesh):
    return jax.shard_map(
        functools.partial(shards, mesh.shape["band"]),
        mesh=mesh,
        in_specs=(
            P(None, "blk", None),
            P("band", None),
            P("blk", None, None),
            P(),
            P(),
            P(),
            P("band", "blk", None),
        ),
        out_specs=P("band", "blk", None),
        check_vma=False,
    )
```

```python
import functools
import math

import jax
import jax.numpy as jnp
from jax import lax
from jax.experimental import pallas as pl
from jax.experimental.pallas import tpu as pltpu
from jax.sharding import PartitionSpec as P

LANES = 128
SLAB = 512
EXTRA = 8
TERMS = 3
VMEM = pltpu.CompilerParams(vmem_limit_bytes=48 * 1024 * 1024)
NT = (((1,), (1,)), ((), ()))


def member_order(blks):
    quarter = blks // 4
    order = [q * quarter + i for q in (2, 3, 1, 0) for i in reversed(range(quarter))]
    return [k for k in order if k % 2 == 1] + [k for k in order if k % 2 == 0]


def synth_kernel(blks, amps_hbm, beam_hbm, leg_hbm, out_ref, amps, beam, leg, weighted, sems):
    degrees = amps.shape[0]
    chunks = amps_hbm.shape[0] // SLAB
    copies = [pltpu.make_async_copy(beam_hbm, beam, sems.at[0])]
    for k in range(chunks):
        at = pl.ds(k * SLAB, SLAB)
        copies.append(pltpu.make_async_copy(amps_hbm.at[at, :], amps.at[at, :], sems.at[1 + 2 * k]))
        copies.append(pltpu.make_async_copy(leg_hbm.at[:, at], leg.at[:, at], sems.at[2 + 2 * k]))
    for copy in copies:
        copy.start()
    copies[0].wait()
    gains = jnp.concatenate(
        [beam[0:1, k * LANES : (k + 1) * LANES] for k in range(degrees // LANES)], axis=0
    ).T
    total = None
    for k in range(chunks):
        copies[1 + 2 * k].wait()
        copies[2 + 2 * k].wait()
        for j in range(k * SLAB, (k + 1) * SLAB, LANES):
            product = amps[j : j + LANES, :].astype(jnp.float32) * gains[:, j // LANES : j // LANES + 1]
            weighted[j : j + LANES, :] = product.astype(jnp.bfloat16)
        at = slice(k * SLAB, (k + 1) * SLAB)
        add = jnp.dot(leg[:, at], weighted[at, :], preferred_element_type=jnp.float32)
        total = add if total is None else total + add
    pair = 2 * total.shape[0] // blks
    for g, k in enumerate(member_order(blks)):
        out_ref[g * pair : (g + 1) * pair, :] = total[k // 2 * pair : (k // 2 + 1) * pair, :]


def mod_exact(value, modulus):
    quotient = (value.astype(jnp.float32) / modulus.astype(jnp.float32)).astype(jnp.int32)
    left = value - quotient * modulus
    left = jnp.where(left < 0, left + modulus, left)
    return jnp.where(left >= modulus, left - modulus, left)


def cos_sin(numer, count):
    countf = count.astype(jnp.float32)
    quarter = ((2 * numer + (count >> 1)).astype(jnp.float32) / countf).astype(jnp.int32)
    rest = (2 * numer - quarter * count).astype(jnp.float32)
    angle = rest * (jnp.float32(math.pi / 2) / countf)
    square = angle * angle
    sin = angle * (
        1.0 + square * (-1.0 / 6 + square * (1.0 / 120 + square * (-1.0 / 5040 + square * (1.0 / 362880))))
    )
    cos = 1.0 + square * (
        -0.5 + square * (1.0 / 24 + square * (-1.0 / 720 + square * (1.0 / 40320 - square * (1.0 / 3628800))))
    )
    odd = (quarter & 1) == 1
    cos_out = jnp.where(odd, sin, cos)
    sin_out = jnp.where(odd, cos, sin)
    cos_out = jnp.where(((quarter + 1) & 2) == 2, -cos_out, cos_out)
    sin_out = jnp.where((quarter & 2) == 2, -sin_out, sin_out)
    return cos_out, sin_out


def gram_kernel(blks, bands, order_ref, cycle_ref, count_ref, noise_ref, beam_ref, keep_ref, give_ref, extra_ref, high, low, whole, lists):
    cycles, pixels = noise_ref.shape
    orders = order_ref.shape[0]
    rows = orders * cycles
    blk = lax.axis_index("blk")
    start = blk * cycles
    row = lax.broadcasted_iota(jnp.int32, (rows, LANES), 0)
    lane = lax.broadcasted_iota(jnp.int32, (rows, LANES), 1)
    slot = row % cycles
    count = jnp.zeros((rows, LANES), jnp.int32)
    parity = jnp.zeros((rows, LANES), jnp.int32)
    for i in range(cycles):
        cycle = cycle_ref[start + i]
        count = jnp.where(slot == i, count_ref[cycle], count)
        parity = jnp.where(slot == i, cycle & 1, parity)
    order = jnp.zeros((rows, LANES), jnp.int32)
    for g, k in enumerate(member_order(blks)):
        order = jnp.where(row // cycles == g, order_ref[k], order)
    fine_c, fine_s = cos_sin(mod_exact(2 * order * lane, 2 * count), count)
    coarse = 2 * LANES * order * (lane & (pixels // LANES - 1)) + order * parity
    coarse_c, coarse_s = cos_sin(mod_exact(coarse, 2 * count), count)
    norm = lax.rsqrt(count.astype(jnp.float32))
    fine_c, fine_s = fine_c * norm, fine_s * norm
    coarse_s = -coarse_s

    pixel = lax.broadcasted_iota(jnp.int32, (cycles, pixels), 1)
    inside = pixel < count[:cycles, :1]
    root = jnp.sqrt(jnp.where(inside, noise_ref[...], 0.0))
    reps = max(8 // cycles, 1)
    root = jnp.concatenate([root] * reps, axis=0)
    period = root.shape[0]

    step = 2
    total = jnp.zeros((2 * rows, 4 * rows), jnp.float32)
    for block in range(pixels // LANES // step):
        for j in range(block * step, (block + 1) * step):
            cols = slice(j * LANES, (j + 1) * LANES)
            here = jnp.concatenate([root[:, cols]] * (rows // period), axis=0)
            a_c, a_s = coarse_c[:, j : j + 1], coarse_s[:, j : j + 1]
            for c, value in enumerate((a_c * fine_c + a_s * fine_s, a_s * fine_c - a_c * fine_s)):
                value = value * here
                top = value.astype(jnp.bfloat16)
                rest = (value - top.astype(jnp.float32)).astype(jnp.bfloat16)
                for p in range(2):
                    to = slice(p * rows + c * (rows // 2), p * rows + (c + 1) * (rows // 2))
                    of = slice(p * (rows // 2), (p + 1) * (rows // 2))
                    high[to, cols] = top[of]
                    low[to, cols] = rest[of]
        cols = slice(block * step * LANES, (block + 1) * step * LANES)
        top = high[:, cols]
        both = jnp.concatenate([top, low[:, cols]], axis=0)
        total = total + lax.dot_general(top, both, NT, preferred_element_type=jnp.float32)
    cross = total[:, 2 * rows :]
    gram = total[:, : 2 * rows] + cross + cross.T
    row = lax.broadcasted_iota(jnp.int32, gram.shape, 0)
    col = lax.broadcasted_iota(jnp.int32, gram.shape, 1)
    gram = jnp.where(row % cycles == col % cycles, gram, 0.0)
    top = gram.astype(jnp.bfloat16)
    rest = (gram - top.astype(jnp.float32)).astype(jnp.bfloat16)
    whole[...] = jnp.concatenate([top, top, rest], axis=1)
    mine = pl.multiple_of((1 - blk % 2) * rows, 16)
    keep_ref[...] = whole[pl.ds(mine, rows), :]
    give_ref[...] = whole[pl.ds(pl.multiple_of(rows - mine, 16), rows), :]

    part = beam_ref.shape[1] // bands
    lines = -(-part // LANES)
    lists[...] = jnp.zeros_like(lists)
    for p in range(bands):
        for t in range(lines):
            size = min(LANES, part - t * LANES)
            first = p * part + t * LANES
            value = beam_ref[0:1, first : first + size]
            for term in range(TERMS):
                top = value.astype(jnp.bfloat16).astype(jnp.float32)
                at = p * (blks // 2) * EXTRA + term * lines + t
                lists[at : at + 1, :size] = top
                value = value - top
        at = pl.multiple_of((p * (blks // 2) + blk // 2) * EXTRA, EXTRA)
        extra_ref[p * EXTRA : (p + 1) * EXTRA, :] = lists[pl.ds(at, EXTRA), :]


def apply_kernel(bands, keep_ref, got_ref, modes_ref, extra_ref, out_ref):
    rows = keep_ref.shape[0]
    pair, width = EXTRA, modes_ref.shape[1]
    chains = width // 2
    first = lax.axis_index("blk") % 2 == 0
    keep, got = keep_ref[...], got_ref[...]
    modes = modes_ref[...].reshape(rows // pair, 2, pair, width)
    even, odd = modes[:, 0], modes[:, 1]
    near = lax.broadcasted_iota(jnp.int32, even.shape, 1) < pair // 2
    halves = []
    for e in range(2):
        if e == 0:
            x = jnp.where(near, even, pltpu.roll(odd, pair // 2, 1))
            matrix = jnp.where(first, keep, got)
        else:
            x = jnp.where(near, pltpu.roll(even, pair // 2, 1), odd)
            matrix = jnp.where(first, got, keep)
        x = x.reshape(rows, width)
        stacked = []
        for p in range(2):
            block = x[p * (rows // 2) : (p + 1) * (rows // 2)]
            stacked += [block[:, :chains], block[:, chains:]]
        stacked = jnp.concatenate(stacked, axis=0)
        top = stacked.astype(jnp.bfloat16)
        rest = (stacked - top.astype(jnp.float32)).astype(jnp.bfloat16)
        right = jnp.concatenate([top, rest, top], axis=0)
        result = jnp.dot(matrix, right, preferred_element_type=jnp.float32)
        half = jnp.concatenate([result[: rows // 2], result[rows // 2 :]], axis=1)
        halves.append(half.reshape(rows // 2 // pair, pair, width))
    near = near[: rows // 2 // pair]
    even = jnp.where(near, halves[0], pltpu.roll(halves[1], pair // 2, 1))
    odd = jnp.where(near, pltpu.roll(halves[0], pair // 2, 1), halves[1])
    size = pair + EXTRA
    for j in range(rows // pair):
        half = (even if j % 2 == 0 else odd)[j // 2]
        for b in range(bands):
            at = (j * bands + bands - 1 - b) * size
            piece = jnp.concatenate([half, extra_ref[b * EXTRA : (b + 1) * EXTRA, :]], axis=0)
            out_ref[at : at + size, :] = piece.astype(jnp.bfloat16)


def turn_kernel(leg_ref, out_ref):
    cycles, part = leg_ref.shape
    for t in range(0, part, LANES):
        size = min(LANES, part - t)
        out_ref[t : t + size, :] = leg_ref[:, t : t + size].astype(jnp.float32).T.astype(jnp.bfloat16)


def analysis_kernel(bands, leg_ref, half_ref, out_hbm, out, sems):
    part, cycles = leg_ref.shape
    width = half_ref.shape[1]
    lines = -(-part // LANES)
    size = 2 * EXTRA
    pairs = half_ref.shape[0] // size // bands
    got = half_ref[...].astype(jnp.float32).reshape(pairs, bands, size, width)
    place = [k // 2 for k in member_order(2 * pairs)[:pairs]]
    place = [place.index(p) for p in range(pairs)]
    right, columns = [], []
    for b in range(bands):
        mine = got[:, bands - 1 - b]
        right.append(jnp.concatenate([mine[place[p], :EXTRA] for p in range(pairs)], axis=0))
        used = -(-TERMS * lines // EXTRA)
        terms = jnp.concatenate([mine[place[p], EXTRA:] for p in range(used)], axis=0)
        gains = terms[:lines]
        for term in range(1, TERMS):
            gains = gains + terms[term * lines : (term + 1) * lines]
        columns.append(gains.T)
    right = jnp.concatenate(right, axis=1).astype(jnp.bfloat16)
    copies = []
    for k in range(len(out_sizes(part))):
        first, many = out_sizes(part)[k]
        product = jnp.dot(leg_ref[first : first + many, :], right, preferred_element_type=jnp.float32)
        for t in range(first, first + many, LANES):
            rows = slice(t, min(t + LANES, part))
            here = product[t - first : t - first + LANES]
            total = None
            for b in range(bands):
                add = columns[b][: here.shape[0], t // LANES : t // LANES + 1] * here[:, b * width : (b + 1) * width]
                total = add if total is None else total + add
            out[rows, :] = total
        at = pl.ds(first, many)
        copies.append(pltpu.make_async_copy(out.at[at, :], out_hbm.at[at, :], sems.at[k]))
        copies[-1].start()
    for copy in copies:
        copy.wait()


def out_sizes(part):
    step = 256
    return [(at, min(step, part - at)) for at in range(0, part, step)]


def shards(bands, amps, beam, legendre, m_values, cycle_order, pixel_counts, inv_noise):
    degrees, _, width = amps.shape
    cycles = legendre.shape[2]
    cycles_here = inv_noise.shape[1]
    orders = m_values.shape[0]
    rows = orders * cycles_here
    part = degrees // bands
    leg = jnp.swapaxes(legendre[0], 0, 1)
    smem = pl.BlockSpec(memory_space=pltpu.SMEM)
    vmem = pl.BlockSpec(memory_space=pltpu.VMEM)

    hbm = pl.BlockSpec(memory_space=pltpu.HBM)
    blks = lax.axis_size("blk")
    pair = 2 * cycles_here
    assert orders == blks and blks % 2 == 0 and pair == EXTRA and cycles == cycles_here * blks
    slabs = degrees // SLAB
    sent = pl.pallas_call(
        functools.partial(synth_kernel, blks),
        out_shape=jax.ShapeDtypeStruct((blks * pair, width), jnp.float32),
        in_specs=[hbm] * 3,
        out_specs=vmem,
        scratch_shapes=[
            pltpu.VMEM((degrees, width), jnp.bfloat16),
            pltpu.VMEM((1, degrees), jnp.float32),
            pltpu.VMEM((cycles, degrees), jnp.bfloat16),
            pltpu.VMEM((degrees, width), jnp.bfloat16),
            pltpu.SemaphoreType.DMA((1 + 2 * slabs,)),
        ],
        compiler_params=pltpu.CompilerParams(vmem_limit_bytes=127 * 512 * 1024),
        cost_estimate=pl.CostEstimate(
            flops=2 * degrees * cycles * width, transcendentals=0, bytes_accessed=2 * degrees * (cycles + width)
        ),
    )(amps[:, 0, :], beam, leg)
    modes = lax.all_to_all(
        sent, "blk", split_axis=0, concat_axis=0, tiled=True, axis_index_groups=[member_order(blks)]
    )

    pixels = inv_noise.shape[2]
    keep, give, extra = pl.pallas_call(
        functools.partial(gram_kernel, blks, bands),
        out_shape=[
            jax.ShapeDtypeStruct((rows, 6 * rows), jnp.bfloat16),
            jax.ShapeDtypeStruct((rows, 6 * rows), jnp.bfloat16),
            jax.ShapeDtypeStruct((bands * EXTRA, LANES), jnp.float32),
        ],
        in_specs=[smem] * 3 + [vmem] * 2,
        out_specs=[vmem] * 3,
        scratch_shapes=[pltpu.VMEM((2 * rows, pixels), jnp.bfloat16)] * 2
        + [
            pltpu.VMEM((2 * rows, 6 * rows), jnp.bfloat16),
            pltpu.VMEM((bands * (blks // 2) * EXTRA, LANES), jnp.float32),
        ],
        compiler_params=VMEM,
        cost_estimate=pl.CostEstimate(
            flops=16 * rows * rows * pixels, transcendentals=0, bytes_accessed=8 * rows * pixels
        ),
    )(m_values, cycle_order, pixel_counts, inv_noise[0], beam)
    got = lax.ppermute(give, "blk", [(k, k ^ 1) for k in range(blks)])

    size = pair + EXTRA
    half = pl.pallas_call(
        functools.partial(apply_kernel, bands),
        out_shape=jax.ShapeDtypeStruct((bands * (blks // 2) * size, width), jnp.bfloat16),
        in_specs=[vmem] * 4,
        out_specs=vmem,
        compiler_params=VMEM,
    )(keep, got, modes, extra)
    half, leg = lax.optimization_barrier((half, leg))
    order = member_order(blks)
    groups = [
        [b * blks + k for k in members for b in reversed(range(bands))]
        for members in (order[: blks // 2], order[blks // 2 :])
    ]
    half = lax.all_to_all(
        half, ("band", "blk"), split_axis=0, concat_axis=0, tiled=True, axis_index_groups=groups
    )

    leg_part = lax.dynamic_slice_in_dim(leg, lax.axis_index("band") * part, part, axis=1)
    leg_turned = pl.pallas_call(
        turn_kernel,
        out_shape=jax.ShapeDtypeStruct((part, cycles), jnp.bfloat16),
        in_specs=[vmem],
        out_specs=vmem,
        compiler_params=VMEM,
        cost_estimate=pl.CostEstimate(flops=part * cycles, transcendentals=0, bytes_accessed=4 * part * cycles),
    )(leg_part)
    out = pl.pallas_call(
        functools.partial(analysis_kernel, bands),
        out_shape=jax.ShapeDtypeStruct((part, width), jnp.float32),
        in_specs=[vmem] * 2,
        out_specs=hbm,
        scratch_shapes=[
            pltpu.VMEM((part, width), jnp.float32),
            pltpu.SemaphoreType.DMA((len(out_sizes(part)),)),
        ],
        compiler_params=VMEM,
    )(leg_turned, half)
    return out[:, None, :]


def solution(mesh):
    return jax.shard_map(
        functools.partial(shards, mesh.shape["band"]),
        mesh=mesh,
        in_specs=(
            P(None, "blk", None),
            P("band", None),
            P("blk", None, None),
            P(),
            P(),
            P(),
            P("band", "blk", None),
        ),
        out_specs=P("band", "blk", None),
        check_vma=False,
    )
```

```python
import functools
import math

import jax
import jax.numpy as jnp
from jax import lax
from jax.experimental import pallas as pl
from jax.experimental.pallas import tpu as pltpu
from jax.sharding import PartitionSpec as P

LANES = 128
SLAB = 1280
EXTRA = 8
TERMS = 3
VMEM = pltpu.CompilerParams(vmem_limit_bytes=48 * 1024 * 1024)
NT = (((1,), (1,)), ((), ()))


def member_order(blks):
    quarter = blks // 4
    order = [q * quarter + i for q in (2, 3, 1, 0) for i in reversed(range(quarter))]
    return [k for k in order if k % 2 == 1] + [k for k in order if k % 2 == 0]


def synth_kernel(blks, amps_hbm, beam_hbm, leg_hbm, out_ref, amps, beam, leg, weighted, sems):
    degrees = amps.shape[0]
    chunks = amps_hbm.shape[0] // SLAB
    copies = [pltpu.make_async_copy(beam_hbm, beam, sems.at[0])]
    for k in range(chunks):
        at = pl.ds(k * SLAB, SLAB)
        copies.append(pltpu.make_async_copy(amps_hbm.at[at, :], amps.at[at, :], sems.at[1 + 2 * k]))
    copies.append(pltpu.make_async_copy(leg_hbm, leg, sems.at[2]))
    for copy in copies:
        copy.start()
    copies[0].wait()
    gains = jnp.concatenate(
        [beam[0:1, k * LANES : (k + 1) * LANES] for k in range(degrees // LANES)], axis=0
    ).T
    for k in range(chunks):
        copies[1 + k].wait()
        for j in range(k * SLAB, (k + 1) * SLAB, LANES):
            product = amps[j : j + LANES, :].astype(jnp.float32) * gains[:, j // LANES : j // LANES + 1]
            weighted[j : j + LANES, :] = product.astype(jnp.bfloat16)
    copies[-1].wait()
    total = jnp.dot(leg[...], weighted[...], preferred_element_type=jnp.float32)
    pair = 2 * total.shape[0] // blks
    for g, k in enumerate(member_order(blks)):
        out_ref[g * pair : (g + 1) * pair, :] = total[k // 2 * pair : (k // 2 + 1) * pair, :]


def mod_exact(value, modulus):
    quotient = (value.astype(jnp.float32) / modulus.astype(jnp.float32)).astype(jnp.int32)
    left = value - quotient * modulus
    left = jnp.where(left < 0, left + modulus, left)
    return jnp.where(left >= modulus, left - modulus, left)


def cos_sin(numer, count):
    countf = count.astype(jnp.float32)
    quarter = ((2 * numer + (count >> 1)).astype(jnp.float32) / countf).astype(jnp.int32)
    rest = (2 * numer - quarter * count).astype(jnp.float32)
    angle = rest * (jnp.float32(math.pi / 2) / countf)
    square = angle * angle
    sin = angle * (
        1.0 + square * (-1.0 / 6 + square * (1.0 / 120 + square * (-1.0 / 5040 + square * (1.0 / 362880))))
    )
    cos = 1.0 + square * (
        -0.5 + square * (1.0 / 24 + square * (-1.0 / 720 + square * (1.0 / 40320 - square * (1.0 / 3628800))))
    )
    odd = (quarter & 1) == 1
    cos_out = jnp.where(odd, sin, cos)
    sin_out = jnp.where(odd, cos, sin)
    cos_out = jnp.where(((quarter + 1) & 2) == 2, -cos_out, cos_out)
    sin_out = jnp.where((quarter & 2) == 2, -sin_out, sin_out)
    return cos_out, sin_out


def gram_kernel(blks, bands, order_ref, cycle_ref, count_ref, noise_ref, beam_ref, keep_ref, give_ref, extra_ref, high, low, whole, lists):
    cycles, pixels = noise_ref.shape
    orders = order_ref.shape[0]
    rows = orders * cycles
    blk = lax.axis_index("blk")
    start = blk * cycles
    row = lax.broadcasted_iota(jnp.int32, (rows, LANES), 0)
    lane = lax.broadcasted_iota(jnp.int32, (rows, LANES), 1)
    slot = row % cycles
    count = jnp.zeros((rows, LANES), jnp.int32)
    parity = jnp.zeros((rows, LANES), jnp.int32)
    for i in range(cycles):
        cycle = cycle_ref[start + i]
        count = jnp.where(slot == i, count_ref[cycle], count)
        parity = jnp.where(slot == i, cycle & 1, parity)
    order = jnp.zeros((rows, LANES), jnp.int32)
    for g, k in enumerate(member_order(blks)):
        order = jnp.where(row // cycles == g, order_ref[k], order)
    fine_c, fine_s = cos_sin(mod_exact(2 * order * lane, 2 * count), count)
    coarse = 2 * LANES * order * (lane & (pixels // LANES - 1)) + order * parity
    coarse_c, coarse_s = cos_sin(mod_exact(coarse, 2 * count), count)
    norm = lax.rsqrt(count.astype(jnp.float32))
    fine_c, fine_s = fine_c * norm, fine_s * norm
    coarse_s = -coarse_s

    pixel = lax.broadcasted_iota(jnp.int32, (cycles, pixels), 1)
    inside = pixel < count[:cycles, :1]
    root = jnp.sqrt(jnp.where(inside, noise_ref[...], 0.0))
    reps = max(8 // cycles, 1)
    root = jnp.concatenate([root] * reps, axis=0)
    period = root.shape[0]

    step = 2
    total = jnp.zeros((2 * rows, 4 * rows), jnp.float32)
    for block in range(pixels // LANES // step):
        for j in range(block * step, (block + 1) * step):
            cols = slice(j * LANES, (j + 1) * LANES)
            here = jnp.concatenate([root[:, cols]] * (rows // period), axis=0)
            a_c, a_s = coarse_c[:, j : j + 1], coarse_s[:, j : j + 1]
            for c, value in enumerate((a_c * fine_c + a_s * fine_s, a_s * fine_c - a_c * fine_s)):
                value = value * here
                top = value.astype(jnp.bfloat16)
                rest = (value - top.astype(jnp.float32)).astype(jnp.bfloat16)
                for p in range(2):
                    to = slice(p * rows + c * (rows // 2), p * rows + (c + 1) * (rows // 2))
                    of = slice(p * (rows // 2), (p + 1) * (rows // 2))
                    high[to, cols] = top[of]
                    low[to, cols] = rest[of]
        cols = slice(block * step * LANES, (block + 1) * step * LANES)
        top = high[:, cols]
        both = jnp.concatenate([top, low[:, cols]], axis=0)
        total = total + lax.dot_general(top, both, NT, preferred_element_type=jnp.float32)
    cross = total[:, 2 * rows :]
    gram = total[:, : 2 * rows] + cross + cross.T
    row = lax.broadcasted_iota(jnp.int32, gram.shape, 0)
    col = lax.broadcasted_iota(jnp.int32, gram.shape, 1)
    gram = jnp.where(row % cycles == col % cycles, gram, 0.0)
    top = gram.astype(jnp.bfloat16)
    rest = (gram - top.astype(jnp.float32)).astype(jnp.bfloat16)
    whole[...] = jnp.concatenate([top, top, rest], axis=1)
    mine = pl.multiple_of((1 - blk % 2) * rows, 16)
    keep_ref[...] = whole[pl.ds(mine, rows), :]
    give_ref[...] = whole[pl.ds(pl.multiple_of(rows - mine, 16), rows), :]

    part = beam_ref.shape[1] // bands
    lines = -(-part // LANES)
    lists[...] = jnp.zeros_like(lists)
    for p in range(bands):
        for t in range(lines):
            size = min(LANES, part - t * LANES)
            first = p * part + t * LANES
            value = beam_ref[0:1, first : first + size]
            for term in range(TERMS):
                top = value.astype(jnp.bfloat16).astype(jnp.float32)
                at = p * (blks // 2) * EXTRA + term * lines + t
                lists[at : at + 1, :size] = top
                value = value - top
        at = pl.multiple_of((p * (blks // 2) + blk // 2) * EXTRA, EXTRA)
        extra_ref[p * EXTRA : (p + 1) * EXTRA, :] = lists[pl.ds(at, EXTRA), :]


def apply_kernel(bands, keep_ref, got_ref, modes_ref, extra_ref, out_ref):
    rows = keep_ref.shape[0]
    pair, width = EXTRA, modes_ref.shape[1]
    chains = width // 2
    first = lax.axis_index("blk") % 2 == 0
    keep, got = keep_ref[...], got_ref[...]
    modes = modes_ref[...].reshape(rows // pair, 2, pair, width)
    even, odd = modes[:, 0], modes[:, 1]
    near = lax.broadcasted_iota(jnp.int32, even.shape, 1) < pair // 2
    halves = []
    for e in range(2):
        if e == 0:
            x = jnp.where(near, even, pltpu.roll(odd, pair // 2, 1))
            matrix = jnp.where(first, keep, got)
        else:
            x = jnp.where(near, pltpu.roll(even, pair // 2, 1), odd)
            matrix = jnp.where(first, got, keep)
        x = x.reshape(rows, width)
        stacked = []
        for p in range(2):
            block = x[p * (rows // 2) : (p + 1) * (rows // 2)]
            stacked += [block[:, :chains], block[:, chains:]]
        stacked = jnp.concatenate(stacked, axis=0)
        top = stacked.astype(jnp.bfloat16)
        rest = (stacked - top.astype(jnp.float32)).astype(jnp.bfloat16)
        right = jnp.concatenate([top, rest, top], axis=0)
        result = jnp.dot(matrix, right, preferred_element_type=jnp.float32)
        half = jnp.concatenate([result[: rows // 2], result[rows // 2 :]], axis=1)
        halves.append(half.reshape(rows // 2 // pair, pair, width))
    near = near[: rows // 2 // pair]
    even = jnp.where(near, halves[0], pltpu.roll(halves[1], pair // 2, 1))
    odd = jnp.where(near, pltpu.roll(halves[0], pair // 2, 1), halves[1])
    size = pair + EXTRA
    for j in range(rows // pair):
        half = (even if j % 2 == 0 else odd)[j // 2]
        for b in range(bands):
            at = (j * bands + bands - 1 - b) * size
            piece = jnp.concatenate([half, extra_ref[b * EXTRA : (b + 1) * EXTRA, :]], axis=0)
            out_ref[at : at + size, :] = piece.astype(jnp.bfloat16)


def turn_kernel(leg_ref, out_ref):
    cycles, part = leg_ref.shape
    for t in range(0, part, LANES):
        size = min(LANES, part - t)
        out_ref[t : t + size, :] = leg_ref[:, t : t + size].astype(jnp.float32).T.astype(jnp.bfloat16)


def analysis_kernel(bands, leg_ref, half_ref, out_hbm, out, sems):
    part, cycles = leg_ref.shape
    width = half_ref.shape[1]
    lines = -(-part // LANES)
    size = 2 * EXTRA
    pairs = half_ref.shape[0] // size // bands
    got = half_ref[...].astype(jnp.float32).reshape(pairs, bands, size, width)
    place = [k // 2 for k in member_order(2 * pairs)[:pairs]]
    place = [place.index(p) for p in range(pairs)]
    right, columns = [], []
    for b in range(bands):
        mine = got[:, bands - 1 - b]
        right.append(jnp.concatenate([mine[place[p], :EXTRA] for p in range(pairs)], axis=0))
        used = -(-TERMS * lines // EXTRA)
        terms = jnp.concatenate([mine[place[p], EXTRA:] for p in range(used)], axis=0)
        gains = terms[:lines]
        for term in range(1, TERMS):
            gains = gains + terms[term * lines : (term + 1) * lines]
        columns.append(gains.T)
    right = jnp.concatenate(right, axis=1).astype(jnp.bfloat16)
    copies = []
    for k in range(len(out_sizes(part))):
        first, many = out_sizes(part)[k]
        product = jnp.dot(leg_ref[first : first + many, :], right, preferred_element_type=jnp.float32)
        for t in range(first, first + many, LANES):
            rows = slice(t, min(t + LANES, part))
            here = product[t - first : t - first + LANES]
            total = None
            for b in range(bands):
                add = columns[b][: here.shape[0], t // LANES : t // LANES + 1] * here[:, b * width : (b + 1) * width]
                total = add if total is None else total + add
            out[rows, :] = total
        at = pl.ds(first, many)
        copies.append(pltpu.make_async_copy(out.at[at, :], out_hbm.at[at, :], sems.at[k]))
        copies[-1].start()
    for copy in copies:
        copy.wait()


def out_sizes(part):
    step = 256
    return [(at, min(step, part - at)) for at in range(0, part, step)]


def shards(bands, amps, beam, legendre, m_values, cycle_order, pixel_counts, inv_noise):
    degrees, _, width = amps.shape
    cycles = legendre.shape[2]
    cycles_here = inv_noise.shape[1]
    orders = m_values.shape[0]
    rows = orders * cycles_here
    part = degrees // bands
    leg = jnp.swapaxes(legendre[0], 0, 1)
    smem = pl.BlockSpec(memory_space=pltpu.SMEM)
    vmem = pl.BlockSpec(memory_space=pltpu.VMEM)

    hbm = pl.BlockSpec(memory_space=pltpu.HBM)
    blks = lax.axis_size("blk")
    pair = 2 * cycles_here
    assert orders == blks and blks % 2 == 0 and pair == EXTRA and cycles == cycles_here * blks
    slabs = degrees // SLAB
    sent = pl.pallas_call(
        functools.partial(synth_kernel, blks),
        out_shape=jax.ShapeDtypeStruct((blks * pair, width), jnp.float32),
        in_specs=[hbm] * 3,
        out_specs=vmem,
        scratch_shapes=[
            pltpu.VMEM((degrees, width), jnp.bfloat16),
            pltpu.VMEM((1, degrees), jnp.float32),
            pltpu.VMEM((cycles, degrees), jnp.bfloat16),
            pltpu.VMEM((degrees, width), jnp.bfloat16),
            pltpu.SemaphoreType.DMA((1 + 2 * slabs,)),
        ],
        compiler_params=pltpu.CompilerParams(vmem_limit_bytes=127 * 512 * 1024),
        cost_estimate=pl.CostEstimate(
            flops=2 * degrees * cycles * width, transcendentals=0, bytes_accessed=2 * degrees * (cycles + width)
        ),
    )(amps[:, 0, :], beam, leg)
    modes = lax.all_to_all(
        sent, "blk", split_axis=0, concat_axis=0, tiled=True, axis_index_groups=[member_order(blks)]
    )

    pixels = inv_noise.shape[2]
    keep, give, extra = pl.pallas_call(
        functools.partial(gram_kernel, blks, bands),
        out_shape=[
            jax.ShapeDtypeStruct((rows, 6 * rows), jnp.bfloat16),
            jax.ShapeDtypeStruct((rows, 6 * rows), jnp.bfloat16),
            jax.ShapeDtypeStruct((bands * EXTRA, LANES), jnp.float32),
        ],
        in_specs=[smem] * 3 + [vmem] * 2,
        out_specs=[vmem] * 3,
        scratch_shapes=[pltpu.VMEM((2 * rows, pixels), jnp.bfloat16)] * 2
        + [
            pltpu.VMEM((2 * rows, 6 * rows), jnp.bfloat16),
            pltpu.VMEM((bands * (blks // 2) * EXTRA, LANES), jnp.float32),
        ],
        compiler_params=VMEM,
        cost_estimate=pl.CostEstimate(
            flops=16 * rows * rows * pixels, transcendentals=0, bytes_accessed=8 * rows * pixels
        ),
    )(m_values, cycle_order, pixel_counts, inv_noise[0], beam)
    got = lax.ppermute(give, "blk", [(k, k ^ 1) for k in range(blks)])

    leg_part = lax.dynamic_slice_in_dim(leg, lax.axis_index("band") * part, part, axis=1)
    leg_turned = pl.pallas_call(
        turn_kernel,
        out_shape=jax.ShapeDtypeStruct((part, cycles), jnp.bfloat16),
        in_specs=[vmem],
        out_specs=vmem,
        compiler_params=VMEM,
        cost_estimate=pl.CostEstimate(flops=part * cycles, transcendentals=0, bytes_accessed=4 * part * cycles),
    )(leg_part)
    size = pair + EXTRA
    half = pl.pallas_call(
        functools.partial(apply_kernel, bands),
        out_shape=jax.ShapeDtypeStruct((bands * (blks // 2) * size, width), jnp.bfloat16),
        in_specs=[vmem] * 4,
        out_specs=vmem,
        compiler_params=VMEM,
    )(keep, got, modes, extra)
    half, leg_turned = lax.optimization_barrier((half, leg_turned))
    order = member_order(blks)
    groups = [
        [b * blks + k for k in members for b in reversed(range(bands))]
        for members in (order[: blks // 2], order[blks // 2 :])
    ]
    half = lax.all_to_all(
        half, ("band", "blk"), split_axis=0, concat_axis=0, tiled=True, axis_index_groups=groups
    )

    out = pl.pallas_call(
        functools.partial(analysis_kernel, bands),
        out_shape=jax.ShapeDtypeStruct((part, width), jnp.float32),
        in_specs=[vmem] * 2,
        out_specs=hbm,
        scratch_shapes=[
            pltpu.VMEM((part, width), jnp.float32),
            pltpu.SemaphoreType.DMA((len(out_sizes(part)),)),
        ],
        compiler_params=VMEM,
    )(leg_turned, half)
    return out[:, None, :]


def solution(mesh):
    return jax.shard_map(
        functools.partial(shards, mesh.shape["band"]),
        mesh=mesh,
        in_specs=(
            P(None, "blk", None),
            P("band", None),
            P("blk", None, None),
            P(),
            P(),
            P(),
            P("band", "blk", None),
        ),
        out_specs=P("band", "blk", None),
        check_vma=False,
    )
```

```python
import functools
import math

import jax
import jax.numpy as jnp
from jax import lax
from jax.experimental import pallas as pl
from jax.experimental.pallas import tpu as pltpu
from jax.sharding import PartitionSpec as P

LANES = 128
SLAB = 1280
EXTRA = 8
TERMS = 3
VMEM = pltpu.CompilerParams(vmem_limit_bytes=48 * 1024 * 1024)
NT = (((1,), (1,)), ((), ()))


def member_order(blks):
    pairs = blks // 2
    quarter = pairs // 4
    order = [q * quarter + i for q in (2, 3, 1, 0) for i in reversed(range(quarter))]
    upper = [int(p >= pairs // 2) for p in range(pairs)]
    return [2 * p + upper[p] for p in order] + [2 * p + 1 - upper[p] for p in order]


def synth_kernel(blks, amps_hbm, beam_hbm, leg_hbm, out_ref, amps, beam, leg, weighted, sems):
    degrees = amps.shape[0]
    chunks = amps_hbm.shape[0] // SLAB
    copies = [pltpu.make_async_copy(beam_hbm, beam, sems.at[0])]
    for k in range(chunks):
        at = pl.ds(k * SLAB, SLAB)
        copies.append(pltpu.make_async_copy(amps_hbm.at[at, :], amps.at[at, :], sems.at[1 + 2 * k]))
    copies.append(pltpu.make_async_copy(leg_hbm, leg, sems.at[2]))
    for copy in copies:
        copy.start()
    copies[0].wait()
    gains = jnp.concatenate(
        [beam[0:1, k * LANES : (k + 1) * LANES] for k in range(degrees // LANES)], axis=0
    ).T
    for k in range(chunks):
        copies[1 + k].wait()
        for j in range(k * SLAB, (k + 1) * SLAB, LANES):
            product = amps[j : j + LANES, :].astype(jnp.float32) * gains[:, j // LANES : j // LANES + 1]
            weighted[j : j + LANES, :] = product.astype(jnp.bfloat16)
    copies[-1].wait()
    total = jnp.dot(leg[...], weighted[...], preferred_element_type=jnp.float32)
    pair = 2 * total.shape[0] // blks
    for g, k in enumerate(member_order(blks)):
        out_ref[g * pair : (g + 1) * pair, :] = total[k // 2 * pair : (k // 2 + 1) * pair, :]


def mod_exact(value, modulus):
    quotient = (value.astype(jnp.float32) / modulus.astype(jnp.float32)).astype(jnp.int32)
    left = value - quotient * modulus
    left = jnp.where(left < 0, left + modulus, left)
    return jnp.where(left >= modulus, left - modulus, left)


def cos_sin(numer, count):
    countf = count.astype(jnp.float32)
    quarter = ((2 * numer + (count >> 1)).astype(jnp.float32) / countf).astype(jnp.int32)
    rest = (2 * numer - quarter * count).astype(jnp.float32)
    angle = rest * (jnp.float32(math.pi / 2) / countf)
    square = angle * angle
    sin = angle * (
        1.0 + square * (-1.0 / 6 + square * (1.0 / 120 + square * (-1.0 / 5040 + square * (1.0 / 362880))))
    )
    cos = 1.0 + square * (
        -0.5 + square * (1.0 / 24 + square * (-1.0 / 720 + square * (1.0 / 40320 - square * (1.0 / 3628800))))
    )
    odd = (quarter & 1) == 1
    cos_out = jnp.where(odd, sin, cos)
    sin_out = jnp.where(odd, cos, sin)
    cos_out = jnp.where(((quarter + 1) & 2) == 2, -cos_out, cos_out)
    sin_out = jnp.where((quarter & 2) == 2, -sin_out, sin_out)
    return cos_out, sin_out


def gram_kernel(blks, bands, order_ref, cycle_ref, count_ref, noise_ref, beam_ref, keep_ref, give_ref, extra_ref, high, low, whole, lists):
    cycles, pixels = noise_ref.shape
    orders = order_ref.shape[0]
    rows = orders * cycles
    blk = lax.axis_index("blk")
    start = blk * cycles
    row = lax.broadcasted_iota(jnp.int32, (rows, LANES), 0)
    lane = lax.broadcasted_iota(jnp.int32, (rows, LANES), 1)
    slot = row % cycles
    count = jnp.zeros((rows, LANES), jnp.int32)
    parity = jnp.zeros((rows, LANES), jnp.int32)
    for i in range(cycles):
        cycle = cycle_ref[start + i]
        count = jnp.where(slot == i, count_ref[cycle], count)
        parity = jnp.where(slot == i, cycle & 1, parity)
    order = jnp.zeros((rows, LANES), jnp.int32)
    for g, k in enumerate(member_order(blks)):
        order = jnp.where(row // cycles == g, order_ref[k], order)
    fine_c, fine_s = cos_sin(mod_exact(2 * order * lane, 2 * count), count)
    coarse = 2 * LANES * order * (lane & (pixels // LANES - 1)) + order * parity
    coarse_c, coarse_s = cos_sin(mod_exact(coarse, 2 * count), count)
    norm = lax.rsqrt(count.astype(jnp.float32))
    fine_c, fine_s = fine_c * norm, fine_s * norm
    coarse_s = -coarse_s

    pixel = lax.broadcasted_iota(jnp.int32, (cycles, pixels), 1)
    inside = pixel < count[:cycles, :1]
    root = jnp.sqrt(jnp.where(inside, noise_ref[...], 0.0))
    reps = max(8 // cycles, 1)
    root = jnp.concatenate([root] * reps, axis=0)
    period = root.shape[0]

    step = 2
    total = jnp.zeros((2 * rows, 4 * rows), jnp.float32)
    for block in range(pixels // LANES // step):
        for j in range(block * step, (block + 1) * step):
            cols = slice(j * LANES, (j + 1) * LANES)
            here = jnp.concatenate([root[:, cols]] * (rows // period), axis=0)
            a_c, a_s = coarse_c[:, j : j + 1], coarse_s[:, j : j + 1]
            for c, value in enumerate((a_c * fine_c + a_s * fine_s, a_s * fine_c - a_c * fine_s)):
                value = value * here
                top = value.astype(jnp.bfloat16)
                rest = (value - top.astype(jnp.float32)).astype(jnp.bfloat16)
                for p in range(2):
                    to = slice(p * rows + c * (rows // 2), p * rows + (c + 1) * (rows // 2))
                    of = slice(p * (rows // 2), (p + 1) * (rows // 2))
                    high[to, cols] = top[of]
                    low[to, cols] = rest[of]
        cols = slice(block * step * LANES, (block + 1) * step * LANES)
        top = high[:, cols]
        both = jnp.concatenate([top, low[:, cols]], axis=0)
        total = total + lax.dot_general(top, both, NT, preferred_element_type=jnp.float32)
    cross = total[:, 2 * rows :]
    gram = total[:, : 2 * rows] + cross + cross.T
    row = lax.broadcasted_iota(jnp.int32, gram.shape, 0)
    col = lax.broadcasted_iota(jnp.int32, gram.shape, 1)
    gram = jnp.where(row % cycles == col % cycles, gram, 0.0)
    top = gram.astype(jnp.bfloat16)
    rest = (gram - top.astype(jnp.float32)).astype(jnp.bfloat16)
    whole[...] = jnp.concatenate([top, top, rest], axis=1)
    upper = (blk // 2 >= blks // 4).astype(jnp.int32)
    mine = pl.multiple_of((blk + upper) % 2 * rows, 16)
    keep_ref[...] = whole[pl.ds(mine, rows), :]
    give_ref[...] = whole[pl.ds(pl.multiple_of(rows - mine, 16), rows), :]

    part = beam_ref.shape[1] // bands
    lines = -(-part // LANES)
    lists[...] = jnp.zeros_like(lists)
    for p in range(bands):
        for t in range(lines):
            size = min(LANES, part - t * LANES)
            first = p * part + t * LANES
            value = beam_ref[0:1, first : first + size]
            for term in range(TERMS):
                top = value.astype(jnp.bfloat16).astype(jnp.float32)
                at = p * (blks // 2) * EXTRA + term * lines + t
                lists[at : at + 1, :size] = top
                value = value - top
        at = pl.multiple_of((p * (blks // 2) + blk // 2) * EXTRA, EXTRA)
        extra_ref[p * EXTRA : (p + 1) * EXTRA, :] = lists[pl.ds(at, EXTRA), :]


def apply_kernel(bands, keep_ref, got_ref, modes_ref, extra_ref, out_ref):
    rows = keep_ref.shape[0]
    pair, width = EXTRA, modes_ref.shape[1]
    chains = width // 2
    first = lax.axis_index("blk") % 2 == 0
    keep, got = keep_ref[...], got_ref[...]
    modes = modes_ref[...].reshape(rows // pair, 2, pair, width)
    even, odd = modes[:, 0], modes[:, 1]
    near = lax.broadcasted_iota(jnp.int32, even.shape, 1) < pair // 2
    halves = []
    for e in range(2):
        if e == 0:
            x = jnp.where(near, even, pltpu.roll(odd, pair // 2, 1))
            matrix = jnp.where(first, keep, got)
        else:
            x = jnp.where(near, pltpu.roll(even, pair // 2, 1), odd)
            matrix = jnp.where(first, got, keep)
        x = x.reshape(rows, width)
        stacked = []
        for p in range(2):
            block = x[p * (rows // 2) : (p + 1) * (rows // 2)]
            stacked += [block[:, :chains], block[:, chains:]]
        stacked = jnp.concatenate(stacked, axis=0)
        top = stacked.astype(jnp.bfloat16)
        rest = (stacked - top.astype(jnp.float32)).astype(jnp.bfloat16)
        right = jnp.concatenate([top, rest, top], axis=0)
        result = jnp.dot(matrix, right, preferred_element_type=jnp.float32)
        half = jnp.concatenate([result[: rows // 2], result[rows // 2 :]], axis=1)
        halves.append(half.reshape(rows // 2 // pair, pair, width))
    near = near[: rows // 2 // pair]
    even = jnp.where(near, halves[0], pltpu.roll(halves[1], pair // 2, 1))
    odd = jnp.where(near, pltpu.roll(halves[0], pair // 2, 1), halves[1])
    size = pair + EXTRA
    for j in range(rows // pair):
        half = (even if j % 2 == 0 else odd)[j // 2]
        for b in range(bands):
            at = (j * bands + bands - 1 - b) * size
            piece = jnp.concatenate([half, extra_ref[b * EXTRA : (b + 1) * EXTRA, :]], axis=0)
            out_ref[at : at + size, :] = piece.astype(jnp.bfloat16)


def turn_kernel(leg_ref, out_ref):
    cycles, part = leg_ref.shape
    for t in range(0, part, LANES):
        size = min(LANES, part - t)
        out_ref[t : t + size, :] = leg_ref[:, t : t + size].astype(jnp.float32).T.astype(jnp.bfloat16)


def analysis_kernel(bands, leg_ref, half_ref, out_hbm, out, sems):
    part, cycles = leg_ref.shape
    width = half_ref.shape[1]
    lines = -(-part // LANES)
    size = 2 * EXTRA
    pairs = half_ref.shape[0] // size // bands
    got = half_ref[...].astype(jnp.float32).reshape(pairs, bands, size, width)
    place = [k // 2 for k in member_order(2 * pairs)[:pairs]]
    place = [place.index(p) for p in range(pairs)]
    right, columns = [], []
    for b in range(bands):
        mine = got[:, bands - 1 - b]
        right.append(jnp.concatenate([mine[place[p], :EXTRA] for p in range(pairs)], axis=0))
        used = -(-TERMS * lines // EXTRA)
        terms = jnp.concatenate([mine[place[p], EXTRA:] for p in range(used)], axis=0)
        gains = terms[:lines]
        for term in range(1, TERMS):
            gains = gains + terms[term * lines : (term + 1) * lines]
        columns.append(gains.T)
    right = jnp.concatenate(right, axis=1).astype(jnp.bfloat16)
    copies = []
    for k in range(len(out_sizes(part))):
        first, many = out_sizes(part)[k]
        product = jnp.dot(leg_ref[first : first + many, :], right, preferred_element_type=jnp.float32)
        for t in range(first, first + many, LANES):
            rows = slice(t, min(t + LANES, part))
            here = product[t - first : t - first + LANES]
            total = None
            for b in range(bands):
                add = columns[b][: here.shape[0], t // LANES : t // LANES + 1] * here[:, b * width : (b + 1) * width]
                total = add if total is None else total + add
            out[rows, :] = total
        at = pl.ds(first, many)
        copies.append(pltpu.make_async_copy(out.at[at, :], out_hbm.at[at, :], sems.at[k]))
        copies[-1].start()
    for copy in copies:
        copy.wait()


def out_sizes(part):
    step = 256
    return [(at, min(step, part - at)) for at in range(0, part, step)]


def shards(bands, amps, beam, legendre, m_values, cycle_order, pixel_counts, inv_noise):
    degrees, _, width = amps.shape
    cycles = legendre.shape[2]
    cycles_here = inv_noise.shape[1]
    orders = m_values.shape[0]
    rows = orders * cycles_here
    part = degrees // bands
    leg = jnp.swapaxes(legendre[0], 0, 1)
    smem = pl.BlockSpec(memory_space=pltpu.SMEM)
    vmem = pl.BlockSpec(memory_space=pltpu.VMEM)

    hbm = pl.BlockSpec(memory_space=pltpu.HBM)
    blks = lax.axis_size("blk")
    pair = 2 * cycles_here
    assert orders == blks and blks % 2 == 0 and pair == EXTRA and cycles == cycles_here * blks
    slabs = degrees // SLAB
    sent = pl.pallas_call(
        functools.partial(synth_kernel, blks),
        out_shape=jax.ShapeDtypeStruct((blks * pair, width), jnp.float32),
        in_specs=[hbm] * 3,
        out_specs=vmem,
        scratch_shapes=[
            pltpu.VMEM((degrees, width), jnp.bfloat16),
            pltpu.VMEM((1, degrees), jnp.float32),
            pltpu.VMEM((cycles, degrees), jnp.bfloat16),
            pltpu.VMEM((degrees, width), jnp.bfloat16),
            pltpu.SemaphoreType.DMA((1 + 2 * slabs,)),
        ],
        compiler_params=pltpu.CompilerParams(vmem_limit_bytes=127 * 512 * 1024),
        cost_estimate=pl.CostEstimate(
            flops=2 * degrees * cycles * width, transcendentals=0, bytes_accessed=2 * degrees * (cycles + width)
        ),
    )(amps[:, 0, :], beam, leg)
    modes = lax.all_to_all(
        sent, "blk", split_axis=0, concat_axis=0, tiled=True, axis_index_groups=[member_order(blks)]
    )

    pixels = inv_noise.shape[2]
    keep, give, extra = pl.pallas_call(
        functools.partial(gram_kernel, blks, bands),
        out_shape=[
            jax.ShapeDtypeStruct((rows, 6 * rows), jnp.bfloat16),
            jax.ShapeDtypeStruct((rows, 6 * rows), jnp.bfloat16),
            jax.ShapeDtypeStruct((bands * EXTRA, LANES), jnp.float32),
        ],
        in_specs=[smem] * 3 + [vmem] * 2,
        out_specs=[vmem] * 3,
        scratch_shapes=[pltpu.VMEM((2 * rows, pixels), jnp.bfloat16)] * 2
        + [
            pltpu.VMEM((2 * rows, 6 * rows), jnp.bfloat16),
            pltpu.VMEM((bands * (blks // 2) * EXTRA, LANES), jnp.float32),
        ],
        compiler_params=VMEM,
        cost_estimate=pl.CostEstimate(
            flops=16 * rows * rows * pixels, transcendentals=0, bytes_accessed=8 * rows * pixels
        ),
    )(m_values, cycle_order, pixel_counts, inv_noise[0], beam)
    got = lax.ppermute(give, "blk", [(k, k ^ 1) for k in range(blks)])

    leg_part = lax.dynamic_slice_in_dim(leg, lax.axis_index("band") * part, part, axis=1)
    leg_turned = pl.pallas_call(
        turn_kernel,
        out_shape=jax.ShapeDtypeStruct((part, cycles), jnp.bfloat16),
        in_specs=[vmem],
        out_specs=vmem,
        compiler_params=VMEM,
        cost_estimate=pl.CostEstimate(flops=part * cycles, transcendentals=0, bytes_accessed=4 * part * cycles),
    )(leg_part)
    size = pair + EXTRA
    half = pl.pallas_call(
        functools.partial(apply_kernel, bands),
        out_shape=jax.ShapeDtypeStruct((bands * (blks // 2) * size, width), jnp.bfloat16),
        in_specs=[vmem] * 4,
        out_specs=vmem,
        compiler_params=VMEM,
    )(keep, got, modes, extra)
    half, leg_turned = lax.optimization_barrier((half, leg_turned))
    order = member_order(blks)
    groups = [
        [b * blks + k for k in members for b in reversed(range(bands))]
        for members in (order[: blks // 2], order[blks // 2 :])
    ]
    half = lax.all_to_all(
        half, ("band", "blk"), split_axis=0, concat_axis=0, tiled=True, axis_index_groups=groups
    )

    out = pl.pallas_call(
        functools.partial(analysis_kernel, bands),
        out_shape=jax.ShapeDtypeStruct((part, width), jnp.float32),
        in_specs=[vmem] * 2,
        out_specs=hbm,
        scratch_shapes=[
            pltpu.VMEM((part, width), jnp.float32),
            pltpu.SemaphoreType.DMA((len(out_sizes(part)),)),
        ],
        compiler_params=VMEM,
    )(leg_turned, half)
    return out[:, None, :]


def solution(mesh):
    return jax.shard_map(
        functools.partial(shards, mesh.shape["band"]),
        mesh=mesh,
        in_specs=(
            P(None, "blk", None),
            P("band", None),
            P("blk", None, None),
            P(),
            P(),
            P(),
            P("band", "blk", None),
        ),
        out_specs=P("band", "blk", None),
        check_vma=False,
    )
```

```python
import functools
import math

import jax
import jax.numpy as jnp
from jax import lax
from jax.experimental import pallas as pl
from jax.experimental.pallas import tpu as pltpu
from jax.sharding import PartitionSpec as P

LANES = 128
SLAB = 1280
EXTRA = 8
TERMS = 3
VMEM = pltpu.CompilerParams(vmem_limit_bytes=48 * 1024 * 1024)
NT = (((1,), (1,)), ((), ()))


def member_order(blks):
    pairs = blks // 2
    quarter = pairs // 4
    order = [q * quarter + i for q in (2, 3, 1, 0) for i in reversed(range(quarter))]
    upper = [int(p >= pairs // 2) for p in range(pairs)]
    return [2 * p + upper[p] for p in order] + [2 * p + 1 - upper[p] for p in order]


def synth_kernel(
    blks, bands, amps_hbm, beam_hbm, leg_hbm, order_hbm, cycle_hbm, count_hbm, noise_hbm,
    out_ref, tables_ref, root_ref, extra_ref,
    amps, beam, leg, weighted, order, cycle, count, noise, lists, sems,
):
    degrees = amps.shape[0]
    cycles, pixels = noise.shape
    chunks = degrees // SLAB
    pairs = [(order_hbm, order), (cycle_hbm, cycle), (count_hbm, count), (beam_hbm, beam), (noise_hbm, noise)]
    for k in range(chunks):
        at = pl.ds(k * SLAB, SLAB)
        pairs.append((amps_hbm.at[at, :], amps.at[at, :]))
    pairs.append((leg_hbm, leg))
    copies = [pltpu.make_async_copy(src, dst, sems.at[n]) for n, (src, dst) in enumerate(pairs)]
    for copy in copies:
        copy.start()
    for copy in copies[:5]:
        copy.wait()
    *tables, counts = phase_tables(blks, pixels, cycles, order, cycle, count)
    tables_ref[...] = jnp.concatenate(tables, axis=0)
    pixel = lax.broadcasted_iota(jnp.int32, noise.shape, 1)
    root = jnp.sqrt(jnp.where(pixel < counts[:cycles, :1], noise[...], 0.0))
    root_ref[...] = jnp.concatenate([root] * (root_ref.shape[0] // cycles), axis=0)
    extra_ref[...] = beam_rows(blks, bands, beam, lists)
    gains = jnp.concatenate(
        [beam[0:1, k * LANES : (k + 1) * LANES] for k in range(degrees // LANES)], axis=0
    ).T
    for k in range(chunks):
        copies[5 + k].wait()
        for j in range(k * SLAB, (k + 1) * SLAB, LANES):
            product = amps[j : j + LANES, :].astype(jnp.float32) * gains[:, j // LANES : j // LANES + 1]
            weighted[j : j + LANES, :] = product.astype(jnp.bfloat16)
    copies[-1].wait()
    total = jnp.dot(leg[...], weighted[...], preferred_element_type=jnp.float32)
    pair = 2 * total.shape[0] // blks
    for g, k in enumerate(member_order(blks)):
        out_ref[g * pair : (g + 1) * pair, :] = total[k // 2 * pair : (k // 2 + 1) * pair, :]


def mod_exact(value, modulus):
    quotient = (value.astype(jnp.float32) / modulus.astype(jnp.float32)).astype(jnp.int32)
    left = value - quotient * modulus
    left = jnp.where(left < 0, left + modulus, left)
    return jnp.where(left >= modulus, left - modulus, left)


def cos_sin(numer, count):
    countf = count.astype(jnp.float32)
    quarter = ((2 * numer + (count >> 1)).astype(jnp.float32) / countf).astype(jnp.int32)
    rest = (2 * numer - quarter * count).astype(jnp.float32)
    angle = rest * (jnp.float32(math.pi / 2) / countf)
    square = angle * angle
    sin = angle * (
        1.0 + square * (-1.0 / 6 + square * (1.0 / 120 + square * (-1.0 / 5040 + square * (1.0 / 362880))))
    )
    cos = 1.0 + square * (
        -0.5 + square * (1.0 / 24 + square * (-1.0 / 720 + square * (1.0 / 40320 - square * (1.0 / 3628800))))
    )
    odd = (quarter & 1) == 1
    cos_out = jnp.where(odd, sin, cos)
    sin_out = jnp.where(odd, cos, sin)
    cos_out = jnp.where(((quarter + 1) & 2) == 2, -cos_out, cos_out)
    sin_out = jnp.where((quarter & 2) == 2, -sin_out, sin_out)
    return cos_out, sin_out


def phase_tables(blks, pixels, cycles, order_ref, cycle_ref, count_ref):
    rows = blks * cycles
    start = lax.axis_index("blk") * cycles
    row = lax.broadcasted_iota(jnp.int32, (rows, LANES), 0)
    lane = lax.broadcasted_iota(jnp.int32, (rows, LANES), 1)
    slot = row % cycles
    count = jnp.zeros((rows, LANES), jnp.int32)
    parity = jnp.zeros((rows, LANES), jnp.int32)
    for i in range(cycles):
        cycle = cycle_ref[start + i]
        count = jnp.where(slot == i, count_ref[cycle], count)
        parity = jnp.where(slot == i, cycle & 1, parity)
    order = jnp.zeros((rows, LANES), jnp.int32)
    for g, k in enumerate(member_order(blks)):
        order = jnp.where(row // cycles == g, order_ref[k], order)
    fine_c, fine_s = cos_sin(mod_exact(2 * order * lane, 2 * count), count)
    coarse = 2 * LANES * order * (lane & (pixels // LANES - 1)) + order * parity
    coarse_c, coarse_s = cos_sin(mod_exact(coarse, 2 * count), count)
    norm = lax.rsqrt(count.astype(jnp.float32))
    return fine_c * norm, fine_s * norm, coarse_c, -coarse_s, count


def beam_rows(blks, bands, beam_ref, lists):
    blk = lax.axis_index("blk")
    part = beam_ref.shape[1] // bands
    lines = -(-part // LANES)
    lists[...] = jnp.zeros_like(lists)
    for p in range(bands):
        for t in range(lines):
            size = min(LANES, part - t * LANES)
            first = p * part + t * LANES
            value = beam_ref[0:1, first : first + size]
            for term in range(TERMS):
                top = value.astype(jnp.bfloat16).astype(jnp.float32)
                at = p * (blks // 2) * EXTRA + term * lines + t
                lists[at : at + 1, :size] = top
                value = value - top
    starts = [pl.multiple_of((p * (blks // 2) + blk // 2) * EXTRA, EXTRA) for p in range(bands)]
    return jnp.concatenate([lists[pl.ds(at, EXTRA), :] for at in starts], axis=0)


def gram_kernel(tables_ref, root_ref, keep_ref, give_ref, high, low, whole):
    blks, blk = lax.axis_size("blk"), lax.axis_index("blk")
    rows = keep_ref.shape[0]
    cycles = rows // blks
    period, pixels = root_ref.shape
    fine_c, fine_s, coarse_c, coarse_s = (tables_ref[k * rows : (k + 1) * rows, :] for k in range(4))
    step = 2
    total = jnp.zeros((2 * rows, 4 * rows), jnp.float32)
    for block in range(pixels // LANES // step):
        for j in range(block * step, (block + 1) * step):
            cols = slice(j * LANES, (j + 1) * LANES)
            here = jnp.concatenate([root_ref[:, cols]] * (rows // period), axis=0)
            a_c, a_s = coarse_c[:, j : j + 1], coarse_s[:, j : j + 1]
            for c, value in enumerate((a_c * fine_c + a_s * fine_s, a_s * fine_c - a_c * fine_s)):
                value = value * here
                top = value.astype(jnp.bfloat16)
                rest = (value - top.astype(jnp.float32)).astype(jnp.bfloat16)
                for p in range(2):
                    to = slice(p * rows + c * (rows // 2), p * rows + (c + 1) * (rows // 2))
                    of = slice(p * (rows // 2), (p + 1) * (rows // 2))
                    high[to, cols] = top[of]
                    low[to, cols] = rest[of]
        cols = slice(block * step * LANES, (block + 1) * step * LANES)
        top = high[:, cols]
        both = jnp.concatenate([top, low[:, cols]], axis=0)
        total = total + lax.dot_general(top, both, NT, preferred_element_type=jnp.float32)
    cross = total[:, 2 * rows :]
    gram = total[:, : 2 * rows] + cross + cross.T
    row = lax.broadcasted_iota(jnp.int32, gram.shape, 0)
    col = lax.broadcasted_iota(jnp.int32, gram.shape, 1)
    gram = jnp.where(row % cycles == col % cycles, gram, 0.0)
    top = gram.astype(jnp.bfloat16)
    rest = (gram - top.astype(jnp.float32)).astype(jnp.bfloat16)
    whole[...] = jnp.concatenate([top, rest], axis=1)
    upper = (blk // 2 >= blks // 4).astype(jnp.int32)
    mine = pl.multiple_of((blk + upper) % 2 * rows, 16)
    keep_ref[...] = whole[pl.ds(mine, rows), :]
    give_ref[...] = whole[pl.ds(pl.multiple_of(rows - mine, 16), rows), :]


def apply_kernel(bands, keep_ref, got_ref, modes_ref, extra_ref, out_ref):
    rows = keep_ref.shape[0]
    terms = keep_ref.shape[1] // 2
    pair, width = EXTRA, modes_ref.shape[1]
    chains = width // 2
    first = lax.axis_index("blk") % 2 == 0
    keep, got = keep_ref[...], got_ref[...]
    modes = modes_ref[...].reshape(rows // pair, 2, pair, width)
    even, odd = modes[:, 0], modes[:, 1]
    near = lax.broadcasted_iota(jnp.int32, even.shape, 1) < pair // 2
    halves = []
    for e in range(2):
        if e == 0:
            x = jnp.where(near, even, pltpu.roll(odd, pair // 2, 1))
            matrix = jnp.where(first, keep, got)
        else:
            x = jnp.where(near, pltpu.roll(even, pair // 2, 1), odd)
            matrix = jnp.where(first, got, keep)
        x = x.reshape(rows, width)
        stacked = []
        for p in range(2):
            block = x[p * (rows // 2) : (p + 1) * (rows // 2)]
            stacked += [block[:, :chains], block[:, chains:]]
        stacked = jnp.concatenate(stacked, axis=0)
        top = stacked.astype(jnp.bfloat16)
        rest = (stacked - top.astype(jnp.float32)).astype(jnp.bfloat16)
        right = jnp.concatenate([top, rest, top], axis=0)
        matrix = jnp.concatenate([matrix[:, :terms], matrix], axis=1)
        result = jnp.dot(matrix, right, preferred_element_type=jnp.float32)
        half = jnp.concatenate([result[: rows // 2], result[rows // 2 :]], axis=1)
        halves.append(half.reshape(rows // 2 // pair, pair, width))
    near = near[: rows // 2 // pair]
    even = jnp.where(near, halves[0], pltpu.roll(halves[1], pair // 2, 1))
    odd = jnp.where(near, pltpu.roll(halves[0], pair // 2, 1), halves[1])
    size = pair + EXTRA
    for j in range(rows // pair):
        half = (even if j % 2 == 0 else odd)[j // 2]
        for b in range(bands):
            at = (j * bands + bands - 1 - b) * size
            piece = jnp.concatenate([half, extra_ref[b * EXTRA : (b + 1) * EXTRA, :]], axis=0)
            out_ref[at : at + size, :] = piece.astype(jnp.bfloat16)


def turn_kernel(leg_ref, out_ref):
    cycles, part = leg_ref.shape
    for t in range(0, part, LANES):
        size = min(LANES, part - t)
        out_ref[t : t + size, :] = leg_ref[:, t : t + size].astype(jnp.float32).T.astype(jnp.bfloat16)


def analysis_kernel(bands, leg_ref, half_ref, out_hbm, out, sems):
    part, cycles = leg_ref.shape
    width = half_ref.shape[1]
    lines = -(-part // LANES)
    size = 2 * EXTRA
    pairs = half_ref.shape[0] // size // bands
    got = half_ref[...].astype(jnp.float32).reshape(pairs, bands, size, width)
    place = [k // 2 for k in member_order(2 * pairs)[:pairs]]
    place = [place.index(p) for p in range(pairs)]
    right, columns = [], []
    for b in range(bands):
        mine = got[:, bands - 1 - b]
        right.append(jnp.concatenate([mine[place[p], :EXTRA] for p in range(pairs)], axis=0))
        used = -(-TERMS * lines // EXTRA)
        terms = jnp.concatenate([mine[place[p], EXTRA:] for p in range(used)], axis=0)
        gains = terms[:lines]
        for term in range(1, TERMS):
            gains = gains + terms[term * lines : (term + 1) * lines]
        columns.append(gains.T)
    right = jnp.concatenate(right, axis=1).astype(jnp.bfloat16)
    copies = []
    for k in range(len(out_sizes(part))):
        first, many = out_sizes(part)[k]
        product = jnp.dot(leg_ref[first : first + many, :], right, preferred_element_type=jnp.float32)
        for t in range(first, first + many, LANES):
            rows = slice(t, min(t + LANES, part))
            here = product[t - first : t - first + LANES]
            total = None
            for b in range(bands):
                add = columns[b][: here.shape[0], t // LANES : t // LANES + 1] * here[:, b * width : (b + 1) * width]
                total = add if total is None else total + add
            out[rows, :] = total
        at = pl.ds(first, many)
        copies.append(pltpu.make_async_copy(out.at[at, :], out_hbm.at[at, :], sems.at[k]))
        copies[-1].start()
    for copy in copies:
        copy.wait()


def out_sizes(part):
    step = 256
    return [(at, min(step, part - at)) for at in range(0, part, step)]


def shards(bands, amps, beam, legendre, m_values, cycle_order, pixel_counts, inv_noise):
    degrees, _, width = amps.shape
    cycles = legendre.shape[2]
    cycles_here = inv_noise.shape[1]
    orders = m_values.shape[0]
    rows = orders * cycles_here
    part = degrees // bands
    leg = jnp.swapaxes(legendre[0], 0, 1)
    vmem = pl.BlockSpec(memory_space=pltpu.VMEM)

    hbm = pl.BlockSpec(memory_space=pltpu.HBM)
    blks = lax.axis_size("blk")
    pair = 2 * cycles_here
    assert orders == blks and blks % 2 == 0 and pair == EXTRA and cycles == cycles_here * blks
    slabs = degrees // SLAB
    pixels = inv_noise.shape[2]
    period = cycles_here * max(8 // cycles_here, 1)
    sent, tables, root, extra = pl.pallas_call(
        functools.partial(synth_kernel, blks, bands),
        out_shape=[
            jax.ShapeDtypeStruct((blks * pair, width), jnp.float32),
            pltpu.VMEM((4 * rows, LANES), jnp.float32),
            pltpu.VMEM((period, pixels), jnp.float32),
            pltpu.VMEM((bands * EXTRA, LANES), jnp.float32),
        ],
        in_specs=[hbm] * 7,
        out_specs=[vmem] * 4,
        scratch_shapes=[
            pltpu.VMEM((degrees, width), jnp.bfloat16),
            pltpu.VMEM((1, degrees), jnp.float32),
            pltpu.VMEM((cycles, degrees), jnp.bfloat16),
            pltpu.VMEM((degrees, width), jnp.bfloat16),
            pltpu.SMEM(m_values.shape, jnp.int32),
            pltpu.SMEM(cycle_order.shape, jnp.int32),
            pltpu.SMEM(pixel_counts.shape, jnp.int32),
            pltpu.VMEM((cycles_here, pixels), jnp.float32),
            pltpu.VMEM((bands * (blks // 2) * EXTRA, LANES), jnp.float32),
            pltpu.SemaphoreType.DMA((6 + slabs,)),
        ],
        compiler_params=pltpu.CompilerParams(vmem_limit_bytes=62 * 1024 * 1024),
        cost_estimate=pl.CostEstimate(
            flops=2000 * degrees * cycles * width, transcendentals=0, bytes_accessed=0
        ),
    )(amps[:, 0, :], beam, leg, m_values, cycle_order, pixel_counts, inv_noise[0])
    modes = lax.all_to_all(
        sent, "blk", split_axis=0, concat_axis=0, tiled=True, axis_index_groups=[member_order(blks)]
    )

    keep, give = pl.pallas_call(
        gram_kernel,
        out_shape=[jax.ShapeDtypeStruct((rows, 4 * rows), jnp.bfloat16)] * 2,
        in_specs=[vmem] * 2,
        out_specs=[vmem] * 2,
        scratch_shapes=[pltpu.VMEM((2 * rows, pixels), jnp.bfloat16)] * 2
        + [pltpu.VMEM((2 * rows, 4 * rows), jnp.bfloat16)],
        compiler_params=VMEM,
        cost_estimate=pl.CostEstimate(
            flops=16 * rows * rows * pixels, transcendentals=0, bytes_accessed=8 * rows * pixels
        ),
    )(tables, root)
    got = lax.ppermute(give, "blk", [(k, k ^ 1) for k in range(blks)])

    leg_part = lax.dynamic_slice_in_dim(leg, lax.axis_index("band") * part, part, axis=1)
    leg_turned = pl.pallas_call(
        turn_kernel,
        out_shape=jax.ShapeDtypeStruct((part, cycles), jnp.bfloat16),
        in_specs=[vmem],
        out_specs=vmem,
        compiler_params=VMEM,
        cost_estimate=pl.CostEstimate(flops=part * cycles, transcendentals=0, bytes_accessed=4 * part * cycles),
    )(leg_part)
    size = pair + EXTRA
    half = pl.pallas_call(
        functools.partial(apply_kernel, bands),
        out_shape=jax.ShapeDtypeStruct((bands * (blks // 2) * size, width), jnp.bfloat16),
        in_specs=[vmem] * 4,
        out_specs=vmem,
        compiler_params=VMEM,
    )(keep, got, modes, extra)
    half, leg_turned = lax.optimization_barrier((half, leg_turned))
    order = member_order(blks)
    groups = [
        [b * blks + k for k in members for b in reversed(range(bands))]
        for members in (order[: blks // 2], order[blks // 2 :])
    ]
    half = lax.all_to_all(
        half, ("band", "blk"), split_axis=0, concat_axis=0, tiled=True, axis_index_groups=groups
    )

    out = pl.pallas_call(
        functools.partial(analysis_kernel, bands),
        out_shape=jax.ShapeDtypeStruct((part, width), jnp.float32),
        in_specs=[vmem] * 2,
        out_specs=hbm,
        scratch_shapes=[
            pltpu.VMEM((part, width), jnp.float32),
            pltpu.SemaphoreType.DMA((len(out_sizes(part)),)),
        ],
        compiler_params=VMEM,
    )(leg_turned, half)
    return out[:, None, :]


def solution(mesh):
    return jax.shard_map(
        functools.partial(shards, mesh.shape["band"]),
        mesh=mesh,
        in_specs=(
            P(None, "blk", None),
            P("band", None),
            P("blk", None, None),
            P(),
            P(),
            P(),
            P("band", "blk", None),
        ),
        out_specs=P("band", "blk", None),
        check_vma=False,
    )
```

```python
import functools
import math

import jax
import jax.numpy as jnp
from jax import lax
from jax.experimental import pallas as pl
from jax.experimental.pallas import tpu as pltpu
from jax.sharding import PartitionSpec as P

LANES = 128
SLAB = 2560
EXTRA = 8
TERMS = 3
VMEM = pltpu.CompilerParams(vmem_limit_bytes=48 * 1024 * 1024)
NT = (((1,), (1,)), ((), ()))


def member_order(blks):
    pairs = blks // 2
    quarter = pairs // 4
    order = [q * quarter + i for q in (2, 3, 1, 0) for i in reversed(range(quarter))]
    upper = [int(p >= pairs // 2) for p in range(pairs)]
    return [2 * p + upper[p] for p in order] + [2 * p + 1 - upper[p] for p in order]


def spread(rows, lines):
    count = rows.shape[0]
    term = lax.broadcasted_iota(jnp.int32, (count, lines * LANES), 0) % lines
    block = lax.broadcasted_iota(jnp.int32, (count, lines * LANES), 1) // LANES
    pick = jnp.where(term == block, 1.0, 0.0).astype(jnp.bfloat16)
    return jnp.dot(rows.T.astype(jnp.bfloat16), pick, preferred_element_type=jnp.float32)


def bf16_terms(value):
    terms = []
    for _ in range(TERMS):
        terms.append(value.astype(jnp.bfloat16).astype(jnp.float32))
        value = value - terms[-1]
    return jnp.concatenate(terms, axis=0)


def synth_kernel(
    blks, bands, amps_hbm, beam_hbm, leg_hbm, order_hbm, cycle_hbm, count_hbm, noise_hbm,
    out_ref, order, cycle, count, noise, extra_ref,
    amps, beam, leg, weighted, wide, lists, sems,
):
    degrees = amps.shape[0]
    chunks = degrees // SLAB
    pairs = [(order_hbm, order), (cycle_hbm, cycle), (count_hbm, count), (beam_hbm, beam), (noise_hbm, noise)]
    for k in range(chunks):
        at = pl.ds(k * SLAB, SLAB)
        pairs.append((amps_hbm.at[at, :], amps.at[at, :]))
    pairs.append((leg_hbm, leg))
    copies = [pltpu.make_async_copy(src, dst, sems.at[n]) for n, (src, dst) in enumerate(pairs)]
    for copy in copies:
        copy.start()
    copies[3].wait()
    lines = degrees // LANES
    rows = jnp.concatenate([beam[0:1, k * LANES : (k + 1) * LANES] for k in range(lines)], axis=0)
    wide[...] = spread(bf16_terms(rows), lines)
    extra_ref[...] = beam_rows(blks, bands, beam, lists)
    for k in range(chunks):
        copies[5 + k].wait()
        for j in range(k * SLAB, (k + 1) * SLAB, LANES):
            product = amps[j : j + LANES, :].astype(jnp.float32) * wide[:, j : j + LANES]
            weighted[j : j + LANES, :] = product.astype(jnp.bfloat16)
    for n in (0, 1, 2, 4, -1):
        copies[n].wait()
    total = jnp.dot(leg[...], weighted[...], preferred_element_type=jnp.float32)
    pair = 2 * total.shape[0] // blks
    for g, k in enumerate(member_order(blks)):
        out_ref[g * pair : (g + 1) * pair, :] = total[k // 2 * pair : (k // 2 + 1) * pair, :]


def mod_exact(value, modulus):
    quotient = (value.astype(jnp.float32) / modulus.astype(jnp.float32)).astype(jnp.int32)
    left = value - quotient * modulus
    left = jnp.where(left < 0, left + modulus, left)
    return jnp.where(left >= modulus, left - modulus, left)


def cos_sin(numer, count):
    countf = count.astype(jnp.float32)
    quarter = ((2 * numer + (count >> 1)).astype(jnp.float32) / countf).astype(jnp.int32)
    rest = (2 * numer - quarter * count).astype(jnp.float32)
    angle = rest * (jnp.float32(math.pi / 2) / countf)
    square = angle * angle
    sin = angle * (
        1.0 + square * (-1.0 / 6 + square * (1.0 / 120 + square * (-1.0 / 5040 + square * (1.0 / 362880))))
    )
    cos = 1.0 + square * (
        -0.5 + square * (1.0 / 24 + square * (-1.0 / 720 + square * (1.0 / 40320 - square * (1.0 / 3628800))))
    )
    odd = (quarter & 1) == 1
    cos_out = jnp.where(odd, sin, cos)
    sin_out = jnp.where(odd, cos, sin)
    cos_out = jnp.where(((quarter + 1) & 2) == 2, -cos_out, cos_out)
    sin_out = jnp.where((quarter & 2) == 2, -sin_out, sin_out)
    return cos_out, sin_out


def phase_tables(blks, pixels, cycles, order_ref, cycle_ref, count_ref):
    rows = blks * cycles
    start = lax.axis_index("blk") * cycles
    row = lax.broadcasted_iota(jnp.int32, (rows, LANES), 0)
    lane = lax.broadcasted_iota(jnp.int32, (rows, LANES), 1)
    slot = row % cycles
    count = jnp.zeros((rows, LANES), jnp.int32)
    parity = jnp.zeros((rows, LANES), jnp.int32)
    for i in range(cycles):
        cycle = cycle_ref[start + i]
        count = jnp.where(slot == i, count_ref[cycle], count)
        parity = jnp.where(slot == i, cycle & 1, parity)
    order = jnp.zeros((rows, LANES), jnp.int32)
    for g, k in enumerate(member_order(blks)):
        order = jnp.where(row // cycles == g, order_ref[k], order)
    fine_c, fine_s = cos_sin(mod_exact(2 * order * lane, 2 * count), count)
    coarse = 2 * LANES * order * (lane & (pixels // LANES - 1)) + order * parity
    coarse_c, coarse_s = cos_sin(mod_exact(coarse, 2 * count), count)
    norm = lax.rsqrt(count.astype(jnp.float32))
    return fine_c * norm, fine_s * norm, coarse_c, -coarse_s, count


def beam_rows(blks, bands, beam_ref, lists):
    blk = lax.axis_index("blk")
    part = beam_ref.shape[1] // bands
    lines = -(-part // LANES)
    lists[...] = jnp.zeros_like(lists)
    for p in range(bands):
        for t in range(lines):
            size = min(LANES, part - t * LANES)
            first = p * part + t * LANES
            value = beam_ref[0:1, first : first + size]
            for term in range(TERMS):
                top = value.astype(jnp.bfloat16).astype(jnp.float32)
                at = p * (blks // 2) * EXTRA + term * lines + t
                lists[at : at + 1, :size] = top
                value = value - top
    starts = [pl.multiple_of((p * (blks // 2) + blk // 2) * EXTRA, EXTRA) for p in range(bands)]
    return jnp.concatenate([lists[pl.ds(at, EXTRA), :] for at in starts], axis=0)


def gram_kernel(order_ref, cycle_ref, count_ref, noise_ref, keep_ref, give_ref, high, low, whole):
    blks, blk = lax.axis_size("blk"), lax.axis_index("blk")
    rows = keep_ref.shape[0]
    cycles = rows // blks
    pixels = noise_ref.shape[1]
    fine_c, fine_s, coarse_c, coarse_s, count = phase_tables(blks, pixels, cycles, order_ref, cycle_ref, count_ref)
    pixel = lax.broadcasted_iota(jnp.int32, noise_ref.shape, 1)
    root = jnp.sqrt(jnp.where(pixel < count[:cycles, :1], noise_ref[...], 0.0))
    root = jnp.concatenate([root] * max(8 // cycles, 1), axis=0)
    period = root.shape[0]
    step = 2
    total = jnp.zeros((2 * rows, 4 * rows), jnp.float32)
    for block in range(pixels // LANES // step):
        for j in range(block * step, (block + 1) * step):
            cols = slice(j * LANES, (j + 1) * LANES)
            here = jnp.concatenate([root[:, cols]] * (rows // period), axis=0)
            a_c, a_s = coarse_c[:, j : j + 1], coarse_s[:, j : j + 1]
            for c, value in enumerate((a_c * fine_c + a_s * fine_s, a_s * fine_c - a_c * fine_s)):
                value = value * here
                top = value.astype(jnp.bfloat16)
                rest = (value - top.astype(jnp.float32)).astype(jnp.bfloat16)
                for p in range(2):
                    to = slice(p * rows + c * (rows // 2), p * rows + (c + 1) * (rows // 2))
                    of = slice(p * (rows // 2), (p + 1) * (rows // 2))
                    high[to, cols] = top[of]
                    low[to, cols] = rest[of]
        cols = slice(block * step * LANES, (block + 1) * step * LANES)
        top = high[:, cols]
        both = jnp.concatenate([top, low[:, cols]], axis=0)
        total = total + lax.dot_general(top, both, NT, preferred_element_type=jnp.float32)
    cross = total[:, 2 * rows :]
    gram = total[:, : 2 * rows] + cross + cross.T
    row = lax.broadcasted_iota(jnp.int32, gram.shape, 0)
    col = lax.broadcasted_iota(jnp.int32, gram.shape, 1)
    gram = jnp.where(row % cycles == col % cycles, gram, 0.0)
    top = gram.astype(jnp.bfloat16)
    rest = (gram - top.astype(jnp.float32)).astype(jnp.bfloat16)
    whole[...] = jnp.concatenate([top, rest], axis=1)
    upper = (blk // 2 >= blks // 4).astype(jnp.int32)
    mine = pl.multiple_of((blk + upper) % 2 * rows, 16)
    keep_ref[...] = whole[pl.ds(mine, rows), :]
    give_ref[...] = whole[pl.ds(pl.multiple_of(rows - mine, 16), rows), :]


def apply_kernel(bands, keep_ref, got_ref, modes_ref, extra_ref, out_ref):
    rows = keep_ref.shape[0]
    terms = keep_ref.shape[1] // 2
    pair, width = EXTRA, modes_ref.shape[1]
    chains = width // 2
    first = lax.axis_index("blk") % 2 == 0
    keep, got = keep_ref[...], got_ref[...]
    modes = modes_ref[...].reshape(rows // pair, 2, pair, width)
    even, odd = modes[:, 0], modes[:, 1]
    near = lax.broadcasted_iota(jnp.int32, even.shape, 1) < pair // 2
    halves = []
    for e in range(2):
        if e == 0:
            x = jnp.where(near, even, pltpu.roll(odd, pair // 2, 1))
            matrix = jnp.where(first, keep, got)
        else:
            x = jnp.where(near, pltpu.roll(even, pair // 2, 1), odd)
            matrix = jnp.where(first, got, keep)
        x = x.reshape(rows, width)
        stacked = []
        for p in range(2):
            block = x[p * (rows // 2) : (p + 1) * (rows // 2)]
            stacked += [block[:, :chains], block[:, chains:]]
        stacked = jnp.concatenate(stacked, axis=0)
        top = stacked.astype(jnp.bfloat16)
        rest = (stacked - top.astype(jnp.float32)).astype(jnp.bfloat16)
        right = jnp.concatenate([top, rest, top], axis=0)
        matrix = jnp.concatenate([matrix[:, :terms], matrix], axis=1)
        result = jnp.dot(matrix, right, preferred_element_type=jnp.float32)
        half = jnp.concatenate([result[: rows // 2], result[rows // 2 :]], axis=1)
        halves.append(half.reshape(rows // 2 // pair, pair, width))
    near = near[: rows // 2 // pair]
    even = jnp.where(near, halves[0], pltpu.roll(halves[1], pair // 2, 1))
    odd = jnp.where(near, pltpu.roll(halves[0], pair // 2, 1), halves[1])
    size = pair + EXTRA
    for j in range(rows // pair):
        half = (even if j % 2 == 0 else odd)[j // 2]
        for b in range(bands):
            at = (j * bands + bands - 1 - b) * size
            piece = jnp.concatenate([half, extra_ref[b * EXTRA : (b + 1) * EXTRA, :]], axis=0)
            out_ref[at : at + size, :] = piece.astype(jnp.bfloat16)


def turn_kernel(leg_ref, out_ref):
    cycles, part = leg_ref.shape
    for t in range(0, part, LANES):
        size = min(LANES, part - t)
        out_ref[t : t + size, :] = leg_ref[:, t : t + size].astype(jnp.float32).T.astype(jnp.bfloat16)


def analysis_kernel(bands, leg_ref, half_ref, out_hbm, out, sems):
    part, cycles = leg_ref.shape
    width = half_ref.shape[1]
    lines = -(-part // LANES)
    size = 2 * EXTRA
    pairs = half_ref.shape[0] // size // bands
    got = half_ref[...].astype(jnp.float32).reshape(pairs, bands, size, width)
    place = [k // 2 for k in member_order(2 * pairs)[:pairs]]
    place = [place.index(p) for p in range(pairs)]
    right, columns = [], []
    for b in range(bands):
        mine = got[:, bands - 1 - b]
        right.append(jnp.concatenate([mine[place[p], :EXTRA] for p in range(pairs)], axis=0))
        used = -(-TERMS * lines // EXTRA)
        terms = jnp.concatenate([mine[place[p], EXTRA:] for p in range(used)], axis=0)
        gains = terms[:lines]
        for term in range(1, TERMS):
            gains = gains + terms[term * lines : (term + 1) * lines]
        columns.append(gains.T)
    right = jnp.concatenate(right, axis=1).astype(jnp.bfloat16)
    copies = []
    for k in range(len(out_sizes(part))):
        first, many = out_sizes(part)[k]
        product = jnp.dot(leg_ref[first : first + many, :], right, preferred_element_type=jnp.float32)
        for t in range(first, first + many, LANES):
            rows = slice(t, min(t + LANES, part))
            here = product[t - first : t - first + LANES]
            total = None
            for b in range(bands):
                add = columns[b][: here.shape[0], t // LANES : t // LANES + 1] * here[:, b * width : (b + 1) * width]
                total = add if total is None else total + add
            out[rows, :] = total
        at = pl.ds(first, many)
        copies.append(pltpu.make_async_copy(out.at[at, :], out_hbm.at[at, :], sems.at[k]))
        copies[-1].start()
    for copy in copies:
        copy.wait()


def out_sizes(part):
    step = 256
    return [(at, min(step, part - at)) for at in range(0, part, step)]


def shards(bands, amps, beam, legendre, m_values, cycle_order, pixel_counts, inv_noise):
    degrees, _, width = amps.shape
    cycles = legendre.shape[2]
    cycles_here = inv_noise.shape[1]
    orders = m_values.shape[0]
    rows = orders * cycles_here
    part = degrees // bands
    leg = jnp.swapaxes(legendre[0], 0, 1)
    smem = pl.BlockSpec(memory_space=pltpu.SMEM)
    vmem = pl.BlockSpec(memory_space=pltpu.VMEM)

    hbm = pl.BlockSpec(memory_space=pltpu.HBM)
    blks = lax.axis_size("blk")
    pair = 2 * cycles_here
    assert orders == blks and blks % 2 == 0 and pair == EXTRA and cycles == cycles_here * blks
    slabs = degrees // SLAB
    pixels = inv_noise.shape[2]
    sent, *gram_inputs, extra = pl.pallas_call(
        functools.partial(synth_kernel, blks, bands),
        out_shape=[
            jax.ShapeDtypeStruct((blks * pair, width), jnp.float32),
            pltpu.VMEM(m_values.shape, jnp.int32),
            pltpu.VMEM(cycle_order.shape, jnp.int32),
            pltpu.VMEM(pixel_counts.shape, jnp.int32),
            pltpu.VMEM((cycles_here, pixels), jnp.float32),
            pltpu.VMEM((bands * EXTRA, LANES), jnp.float32),
        ],
        in_specs=[hbm] * 7,
        out_specs=[vmem] * 6,
        scratch_shapes=[
            pltpu.VMEM((degrees, width), jnp.bfloat16),
            pltpu.VMEM((1, degrees), jnp.float32),
            pltpu.VMEM((cycles, degrees), jnp.bfloat16),
            pltpu.VMEM((degrees, width), jnp.bfloat16),
            pltpu.VMEM((LANES, degrees), jnp.float32),
            pltpu.VMEM((bands * (blks // 2) * EXTRA, LANES), jnp.float32),
            pltpu.SemaphoreType.DMA((6 + slabs,)),
        ],
        compiler_params=pltpu.CompilerParams(vmem_limit_bytes=62 * 1024 * 1024),
        cost_estimate=pl.CostEstimate(
            flops=2000 * degrees * cycles * width, transcendentals=0, bytes_accessed=0
        ),
    )(amps[:, 0, :], beam, leg, m_values, cycle_order, pixel_counts, inv_noise[0])
    modes = lax.all_to_all(
        sent, "blk", split_axis=0, concat_axis=0, tiled=True, axis_index_groups=[member_order(blks)]
    )

    keep, give = pl.pallas_call(
        gram_kernel,
        out_shape=[jax.ShapeDtypeStruct((rows, 4 * rows), jnp.bfloat16)] * 2,
        in_specs=[smem] * 3 + [vmem],
        out_specs=[vmem] * 2,
        scratch_shapes=[pltpu.VMEM((2 * rows, pixels), jnp.bfloat16)] * 2
        + [pltpu.VMEM((2 * rows, 4 * rows), jnp.bfloat16)],
        compiler_params=VMEM,
        cost_estimate=pl.CostEstimate(
            flops=16 * rows * rows * pixels, transcendentals=0, bytes_accessed=8 * rows * pixels
        ),
    )(*gram_inputs)
    got = lax.ppermute(give, "blk", [(k, k ^ 1) for k in range(blks)])

    leg_part = lax.dynamic_slice_in_dim(leg, lax.axis_index("band") * part, part, axis=1)
    leg_turned = pl.pallas_call(
        turn_kernel,
        out_shape=jax.ShapeDtypeStruct((part, cycles), jnp.bfloat16),
        in_specs=[vmem],
        out_specs=vmem,
        compiler_params=VMEM,
        cost_estimate=pl.CostEstimate(flops=part * cycles, transcendentals=0, bytes_accessed=4 * part * cycles),
    )(leg_part)
    size = pair + EXTRA
    half = pl.pallas_call(
        functools.partial(apply_kernel, bands),
        out_shape=jax.ShapeDtypeStruct((bands * (blks // 2) * size, width), jnp.bfloat16),
        in_specs=[vmem] * 4,
        out_specs=vmem,
        compiler_params=VMEM,
    )(keep, got, modes, extra)
    half, leg_turned = lax.optimization_barrier((half, leg_turned))
    order = member_order(blks)
    groups = [
        [b * blks + k for k in members for b in reversed(range(bands))]
        for members in (order[: blks // 2], order[blks // 2 :])
    ]
    half = lax.all_to_all(
        half, ("band", "blk"), split_axis=0, concat_axis=0, tiled=True, axis_index_groups=groups
    )

    out = pl.pallas_call(
        functools.partial(analysis_kernel, bands),
        out_shape=jax.ShapeDtypeStruct((part, width), jnp.float32),
        in_specs=[vmem] * 2,
        out_specs=hbm,
        scratch_shapes=[
            pltpu.VMEM((part, width), jnp.float32),
            pltpu.SemaphoreType.DMA((len(out_sizes(part)),)),
        ],
        compiler_params=VMEM,
    )(leg_turned, half)
    return out[:, None, :]


def solution(mesh):
    return jax.shard_map(
        functools.partial(shards, mesh.shape["band"]),
        mesh=mesh,
        in_specs=(
            P(None, "blk", None),
            P("band", None),
            P("blk", None, None),
            P(),
            P(),
            P(),
            P("band", "blk", None),
        ),
        out_specs=P("band", "blk", None),
        check_vma=False,
    )
```

```python
import functools
import math

import jax
import jax.numpy as jnp
from jax import lax
from jax.experimental import pallas as pl
from jax.experimental.pallas import tpu as pltpu
from jax.sharding import PartitionSpec as P

LANES = 128
SLAB = 2560
EXTRA = 8
TERMS = 3
VMEM = pltpu.CompilerParams(vmem_limit_bytes=48 * 1024 * 1024)
NT = (((1,), (1,)), ((), ()))


def member_order(blks):
    pairs = blks // 2
    quarter = pairs // 4
    order = [q * quarter + i for q in (2, 3, 1, 0) for i in reversed(range(quarter))]
    upper = [int(p >= pairs // 2) for p in range(pairs)]
    return [2 * p + upper[p] for p in order] + [2 * p + 1 - upper[p] for p in order]


def spread(rows, lines):
    count = rows.shape[0]
    term = lax.broadcasted_iota(jnp.int32, (count, lines * LANES), 0) % lines
    block = lax.broadcasted_iota(jnp.int32, (count, lines * LANES), 1) // LANES
    pick = jnp.where(term == block, 1.0, 0.0).astype(jnp.bfloat16)
    return jnp.dot(rows.T.astype(jnp.bfloat16), pick, preferred_element_type=jnp.float32)


def bf16_terms(value):
    terms = []
    for _ in range(TERMS):
        terms.append(value.astype(jnp.bfloat16).astype(jnp.float32))
        value = value - terms[-1]
    return jnp.concatenate(terms, axis=0)


def synth_kernel(
    blks, bands, amps_hbm, beam_hbm, leg_hbm, order_hbm, cycle_hbm, count_hbm, noise_hbm,
    out_ref, order, cycle, count, noise, extra_ref,
    amps, beam, leg, weighted, wide, lists, sems,
):
    degrees = amps.shape[0]
    chunks = degrees // SLAB
    pairs = [(order_hbm, order), (cycle_hbm, cycle), (count_hbm, count), (beam_hbm, beam), (noise_hbm, noise)]
    for k in range(chunks):
        at = pl.ds(k * SLAB, SLAB)
        pairs.append((amps_hbm.at[at, :], amps.at[at, :]))
    pairs.append((leg_hbm, leg))
    copies = [pltpu.make_async_copy(src, dst, sems.at[n]) for n, (src, dst) in enumerate(pairs)]
    for copy in copies[3:4] + copies[5:] + copies[:3] + copies[4:5]:
        copy.start()
    copies[3].wait()
    lines = degrees // LANES
    rows = jnp.concatenate([beam[0:1, k * LANES : (k + 1) * LANES] for k in range(lines)], axis=0)
    wide[...] = spread(bf16_terms(rows), lines)
    extra_ref[...] = beam_rows(blks, bands, beam, lists)
    for k in range(chunks):
        copies[5 + k].wait()
        for j in range(k * SLAB, (k + 1) * SLAB, LANES):
            product = amps[j : j + LANES, :].astype(jnp.float32) * wide[:, j : j + LANES]
            weighted[j : j + LANES, :] = product.astype(jnp.bfloat16)
    for n in (0, 1, 2, 4, -1):
        copies[n].wait()
    total = jnp.dot(leg[...], weighted[...], preferred_element_type=jnp.float32)
    pair = 2 * total.shape[0] // blks
    for g, k in enumerate(member_order(blks)):
        out_ref[g * pair : (g + 1) * pair, :] = total[k // 2 * pair : (k // 2 + 1) * pair, :]


def mod_exact(value, modulus):
    quotient = (value.astype(jnp.float32) / modulus.astype(jnp.float32)).astype(jnp.int32)
    left = value - quotient * modulus
    left = jnp.where(left < 0, left + modulus, left)
    return jnp.where(left >= modulus, left - modulus, left)


def cos_sin(numer, count):
    countf = count.astype(jnp.float32)
    quarter = ((2 * numer + (count >> 1)).astype(jnp.float32) / countf).astype(jnp.int32)
    rest = (2 * numer - quarter * count).astype(jnp.float32)
    angle = rest * (jnp.float32(math.pi / 2) / countf)
    square = angle * angle
    sin = angle * (
        1.0 + square * (-1.0 / 6 + square * (1.0 / 120 + square * (-1.0 / 5040 + square * (1.0 / 362880))))
    )
    cos = 1.0 + square * (
        -0.5 + square * (1.0 / 24 + square * (-1.0 / 720 + square * (1.0 / 40320 - square * (1.0 / 3628800))))
    )
    odd = (quarter & 1) == 1
    cos_out = jnp.where(odd, sin, cos)
    sin_out = jnp.where(odd, cos, sin)
    cos_out = jnp.where(((quarter + 1) & 2) == 2, -cos_out, cos_out)
    sin_out = jnp.where((quarter & 2) == 2, -sin_out, sin_out)
    return cos_out, sin_out


def phase_tables(blks, pixels, cycles, order_ref, cycle_ref, count_ref):
    rows = blks * cycles
    start = lax.axis_index("blk") * cycles
    row = lax.broadcasted_iota(jnp.int32, (rows, LANES), 0)
    lane = lax.broadcasted_iota(jnp.int32, (rows, LANES), 1)
    slot = row % cycles
    count = jnp.zeros((rows, LANES), jnp.int32)
    parity = jnp.zeros((rows, LANES), jnp.int32)
    for i in range(cycles):
        cycle = cycle_ref[start + i]
        count = jnp.where(slot == i, count_ref[cycle], count)
        parity = jnp.where(slot == i, cycle & 1, parity)
    order = jnp.zeros((rows, LANES), jnp.int32)
    for g, k in enumerate(member_order(blks)):
        order = jnp.where(row // cycles == g, order_ref[k], order)
    fine_c, fine_s = cos_sin(mod_exact(2 * order * lane, 2 * count), count)
    coarse = 2 * LANES * order * (lane & (pixels // LANES - 1)) + order * parity
    coarse_c, coarse_s = cos_sin(mod_exact(coarse, 2 * count), count)
    norm = lax.rsqrt(count.astype(jnp.float32))
    return fine_c * norm, fine_s * norm, coarse_c, -coarse_s, count


def beam_rows(blks, bands, beam_ref, lists):
    blk = lax.axis_index("blk")
    part = beam_ref.shape[1] // bands
    lines = -(-part // LANES)
    lists[...] = jnp.zeros_like(lists)
    for p in range(bands):
        for t in range(lines):
            size = min(LANES, part - t * LANES)
            first = p * part + t * LANES
            value = beam_ref[0:1, first : first + size]
            for term in range(TERMS):
                top = value.astype(jnp.bfloat16).astype(jnp.float32)
                at = p * (blks // 2) * EXTRA + term * lines + t
                lists[at : at + 1, :size] = top
                value = value - top
    starts = [pl.multiple_of((p * (blks // 2) + blk // 2) * EXTRA, EXTRA) for p in range(bands)]
    return jnp.concatenate([lists[pl.ds(at, EXTRA), :] for at in starts], axis=0)


def gram_kernel(order_ref, cycle_ref, count_ref, noise_ref, keep_ref, give_ref, high, low, whole):
    blks, blk = lax.axis_size("blk"), lax.axis_index("blk")
    rows = keep_ref.shape[0]
    cycles = rows // blks
    pixels = noise_ref.shape[1]
    fine_c, fine_s, coarse_c, coarse_s, count = phase_tables(blks, pixels, cycles, order_ref, cycle_ref, count_ref)
    pixel = lax.broadcasted_iota(jnp.int32, noise_ref.shape, 1)
    root = jnp.sqrt(jnp.where(pixel < count[:cycles, :1], noise_ref[...], 0.0))
    root = jnp.concatenate([root] * max(8 // cycles, 1), axis=0)
    period = root.shape[0]
    step = 2
    total = jnp.zeros((2 * rows, 4 * rows), jnp.float32)
    for block in range(pixels // LANES // step):
        for j in range(block * step, (block + 1) * step):
            cols = slice(j * LANES, (j + 1) * LANES)
            here = jnp.concatenate([root[:, cols]] * (rows // period), axis=0)
            a_c, a_s = coarse_c[:, j : j + 1], coarse_s[:, j : j + 1]
            for c, value in enumerate((a_c * fine_c + a_s * fine_s, a_s * fine_c - a_c * fine_s)):
                value = value * here
                top = value.astype(jnp.bfloat16)
                rest = (value - top.astype(jnp.float32)).astype(jnp.bfloat16)
                for p in range(2):
                    to = slice(p * rows + c * (rows // 2), p * rows + (c + 1) * (rows // 2))
                    of = slice(p * (rows // 2), (p + 1) * (rows // 2))
                    high[to, cols] = top[of]
                    low[to, cols] = rest[of]
        cols = slice(block * step * LANES, (block + 1) * step * LANES)
        top = high[:, cols]
        both = jnp.concatenate([top, low[:, cols]], axis=0)
        total = total + lax.dot_general(top, both, NT, preferred_element_type=jnp.float32)
    cross = total[:, 2 * rows :]
    gram = total[:, : 2 * rows] + cross + cross.T
    row = lax.broadcasted_iota(jnp.int32, gram.shape, 0)
    col = lax.broadcasted_iota(jnp.int32, gram.shape, 1)
    gram = jnp.where(row % cycles == col % cycles, gram, 0.0)
    top = gram.astype(jnp.bfloat16)
    rest = (gram - top.astype(jnp.float32)).astype(jnp.bfloat16)
    whole[...] = jnp.concatenate([top, rest], axis=1)
    upper = (blk // 2 >= blks // 4).astype(jnp.int32)
    mine = pl.multiple_of((blk + upper) % 2 * rows, 16)
    keep_ref[...] = whole[pl.ds(mine, rows), :]
    give_ref[...] = whole[pl.ds(pl.multiple_of(rows - mine, 16), rows), :]


def apply_kernel(bands, keep_ref, got_ref, modes_ref, extra_ref, out_ref):
    rows = keep_ref.shape[0]
    terms = keep_ref.shape[1] // 2
    pair, width = EXTRA, modes_ref.shape[1]
    chains = width // 2
    first = lax.axis_index("blk") % 2 == 0
    keep, got = keep_ref[...], got_ref[...]
    modes = modes_ref[...].reshape(rows // pair, 2, pair, width)
    even, odd = modes[:, 0], modes[:, 1]
    near = lax.broadcasted_iota(jnp.int32, even.shape, 1) < pair // 2
    halves = []
    for e in range(2):
        if e == 0:
            x = jnp.where(near, even, pltpu.roll(odd, pair // 2, 1))
            matrix = jnp.where(first, keep, got)
        else:
            x = jnp.where(near, pltpu.roll(even, pair // 2, 1), odd)
            matrix = jnp.where(first, got, keep)
        x = x.reshape(rows, width)
        stacked = []
        for p in range(2):
            block = x[p * (rows // 2) : (p + 1) * (rows // 2)]
            stacked += [block[:, :chains], block[:, chains:]]
        stacked = jnp.concatenate(stacked, axis=0)
        top = stacked.astype(jnp.bfloat16)
        rest = (stacked - top.astype(jnp.float32)).astype(jnp.bfloat16)
        right = jnp.concatenate([top, rest, top], axis=0)
        matrix = jnp.concatenate([matrix[:, :terms], matrix], axis=1)
        result = jnp.dot(matrix, right, preferred_element_type=jnp.float32)
        half = jnp.concatenate([result[: rows // 2], result[rows // 2 :]], axis=1)
        halves.append(half.reshape(rows // 2 // pair, pair, width))
    near = near[: rows // 2 // pair]
    even = jnp.where(near, halves[0], pltpu.roll(halves[1], pair // 2, 1))
    odd = jnp.where(near, pltpu.roll(halves[0], pair // 2, 1), halves[1])
    size = pair + EXTRA
    for j in range(rows // pair):
        half = (even if j % 2 == 0 else odd)[j // 2]
        for b in range(bands):
            at = (j * bands + bands - 1 - b) * size
            piece = jnp.concatenate([half, extra_ref[b * EXTRA : (b + 1) * EXTRA, :]], axis=0)
            out_ref[at : at + size, :] = piece.astype(jnp.bfloat16)


def turn_kernel(leg_ref, out_ref):
    cycles, part = leg_ref.shape
    for t in range(0, part, LANES):
        size = min(LANES, part - t)
        out_ref[t : t + size, :] = leg_ref[:, t : t + size].astype(jnp.float32).T.astype(jnp.bfloat16)


def analysis_kernel(bands, leg_ref, half_ref, out_hbm, out, sems):
    part, cycles = leg_ref.shape
    width = half_ref.shape[1]
    lines = -(-part // LANES)
    size = 2 * EXTRA
    pairs = half_ref.shape[0] // size // bands
    got = half_ref[...].astype(jnp.float32).reshape(pairs, bands, size, width)
    place = [k // 2 for k in member_order(2 * pairs)[:pairs]]
    place = [place.index(p) for p in range(pairs)]
    right, columns = [], []
    for b in range(bands):
        mine = got[:, bands - 1 - b]
        right.append(jnp.concatenate([mine[place[p], :EXTRA] for p in range(pairs)], axis=0))
        used = -(-TERMS * lines // EXTRA)
        terms = jnp.concatenate([mine[place[p], EXTRA:] for p in range(used)], axis=0)
        gains = terms[:lines]
        for term in range(1, TERMS):
            gains = gains + terms[term * lines : (term + 1) * lines]
        columns.append(gains.T)
    right = jnp.concatenate(right, axis=1).astype(jnp.bfloat16)
    copies = []
    for k in range(len(out_sizes(part))):
        first, many = out_sizes(part)[k]
        product = jnp.dot(leg_ref[first : first + many, :], right, preferred_element_type=jnp.float32)
        for t in range(first, first + many, LANES):
            rows = slice(t, min(t + LANES, part))
            here = product[t - first : t - first + LANES]
            total = None
            for b in range(bands):
                add = columns[b][: here.shape[0], t // LANES : t // LANES + 1] * here[:, b * width : (b + 1) * width]
                total = add if total is None else total + add
            out[rows, :] = total
        at = pl.ds(first, many)
        copies.append(pltpu.make_async_copy(out.at[at, :], out_hbm.at[at, :], sems.at[k]))
        copies[-1].start()
    for copy in copies:
        copy.wait()


def out_sizes(part):
    step = 256
    return [(at, min(step, part - at)) for at in range(0, part, step)]


def shards(bands, amps, beam, legendre, m_values, cycle_order, pixel_counts, inv_noise):
    degrees, _, width = amps.shape
    cycles = legendre.shape[2]
    cycles_here = inv_noise.shape[1]
    orders = m_values.shape[0]
    rows = orders * cycles_here
    part = degrees // bands
    leg = jnp.swapaxes(legendre[0], 0, 1)
    smem = pl.BlockSpec(memory_space=pltpu.SMEM)
    vmem = pl.BlockSpec(memory_space=pltpu.VMEM)

    hbm = pl.BlockSpec(memory_space=pltpu.HBM)
    blks = lax.axis_size("blk")
    pair = 2 * cycles_here
    assert orders == blks and blks % 2 == 0 and pair == EXTRA and cycles == cycles_here * blks
    slabs = degrees // SLAB
    pixels = inv_noise.shape[2]
    sent, *gram_inputs, extra = pl.pallas_call(
        functools.partial(synth_kernel, blks, bands),
        out_shape=[
            jax.ShapeDtypeStruct((blks * pair, width), jnp.float32),
            pltpu.VMEM(m_values.shape, jnp.int32),
            pltpu.VMEM(cycle_order.shape, jnp.int32),
            pltpu.VMEM(pixel_counts.shape, jnp.int32),
            pltpu.VMEM((cycles_here, pixels), jnp.float32),
            pltpu.VMEM((bands * EXTRA, LANES), jnp.float32),
        ],
        in_specs=[hbm] * 7,
        out_specs=[vmem] * 6,
        scratch_shapes=[
            pltpu.VMEM((degrees, width), jnp.bfloat16),
            pltpu.VMEM((1, degrees), jnp.float32),
            pltpu.VMEM((cycles, degrees), jnp.bfloat16),
            pltpu.VMEM((degrees, width), jnp.bfloat16),
            pltpu.VMEM((LANES, degrees), jnp.float32),
            pltpu.VMEM((bands * (blks // 2) * EXTRA, LANES), jnp.float32),
            pltpu.SemaphoreType.DMA((6 + slabs,)),
        ],
        compiler_params=pltpu.CompilerParams(vmem_limit_bytes=62 * 1024 * 1024),
        cost_estimate=pl.CostEstimate(
            flops=2000 * degrees * cycles * width, transcendentals=0, bytes_accessed=0
        ),
    )(amps[:, 0, :], beam, leg, m_values, cycle_order, pixel_counts, inv_noise[0])
    modes = lax.all_to_all(
        sent, "blk", split_axis=0, concat_axis=0, tiled=True, axis_index_groups=[member_order(blks)]
    )

    keep, give = pl.pallas_call(
        gram_kernel,
        out_shape=[jax.ShapeDtypeStruct((rows, 4 * rows), jnp.bfloat16)] * 2,
        in_specs=[smem] * 3 + [vmem],
        out_specs=[vmem] * 2,
        scratch_shapes=[pltpu.VMEM((2 * rows, pixels), jnp.bfloat16)] * 2
        + [pltpu.VMEM((2 * rows, 4 * rows), jnp.bfloat16)],
        compiler_params=VMEM,
        cost_estimate=pl.CostEstimate(
            flops=16 * rows * rows * pixels, transcendentals=0, bytes_accessed=8 * rows * pixels
        ),
    )(*gram_inputs)
    got = lax.ppermute(give, "blk", [(k, k ^ 1) for k in range(blks)])

    leg_part = lax.dynamic_slice_in_dim(leg, lax.axis_index("band") * part, part, axis=1)
    leg_turned = pl.pallas_call(
        turn_kernel,
        out_shape=jax.ShapeDtypeStruct((part, cycles), jnp.bfloat16),
        in_specs=[vmem],
        out_specs=vmem,
        compiler_params=VMEM,
        cost_estimate=pl.CostEstimate(flops=part * cycles, transcendentals=0, bytes_accessed=4 * part * cycles),
    )(leg_part)
    size = pair + EXTRA
    half = pl.pallas_call(
        functools.partial(apply_kernel, bands),
        out_shape=jax.ShapeDtypeStruct((bands * (blks // 2) * size, width), jnp.bfloat16),
        in_specs=[vmem] * 4,
        out_specs=vmem,
        compiler_params=VMEM,
    )(keep, got, modes, extra)
    half, leg_turned = lax.optimization_barrier((half, leg_turned))
    order = member_order(blks)
    groups = [
        [b * blks + k for k in members for b in reversed(range(bands))]
        for members in (order[: blks // 2], order[blks // 2 :])
    ]
    half = lax.all_to_all(
        half, ("band", "blk"), split_axis=0, concat_axis=0, tiled=True, axis_index_groups=groups
    )

    out = pl.pallas_call(
        functools.partial(analysis_kernel, bands),
        out_shape=jax.ShapeDtypeStruct((part, width), jnp.float32),
        in_specs=[vmem] * 2,
        out_specs=hbm,
        scratch_shapes=[
            pltpu.VMEM((part, width), jnp.float32),
            pltpu.SemaphoreType.DMA((len(out_sizes(part)),)),
        ],
        compiler_params=VMEM,
    )(leg_turned, half)
    return out[:, None, :]


def solution(mesh):
    return jax.shard_map(
        functools.partial(shards, mesh.shape["band"]),
        mesh=mesh,
        in_specs=(
            P(None, "blk", None),
            P("band", None),
            P("blk", None, None),
            P(),
            P(),
            P(),
            P("band", "blk", None),
        ),
        out_specs=P("band", "blk", None),
        check_vma=False,
    )
```

```python
import functools
import math

import jax
import jax.numpy as jnp
from jax import lax
from jax.experimental import pallas as pl
from jax.experimental.pallas import tpu as pltpu
from jax.sharding import PartitionSpec as P

LANES = 128
SLAB = 1280
EXTRA = 8
TERMS = 3
VMEM = pltpu.CompilerParams(vmem_limit_bytes=48 * 1024 * 1024)
NT = (((1,), (1,)), ((), ()))


def member_order(blks):
    pairs = blks // 2
    quarter = pairs // 4
    order = [q * quarter + i for q in (2, 3, 1, 0) for i in reversed(range(quarter))]
    upper = [int(p >= pairs // 2) for p in range(pairs)]
    return [2 * p + upper[p] for p in order] + [2 * p + 1 - upper[p] for p in order]


def spread(rows, lines):
    count = rows.shape[0]
    term = lax.broadcasted_iota(jnp.int32, (count, lines * LANES), 0) % lines
    block = lax.broadcasted_iota(jnp.int32, (count, lines * LANES), 1) // LANES
    pick = jnp.where(term == block, 1.0, 0.0).astype(jnp.bfloat16)
    return jnp.dot(rows.T.astype(jnp.bfloat16), pick, preferred_element_type=jnp.float32)


def bf16_terms(value):
    terms = []
    for _ in range(TERMS):
        terms.append(value.astype(jnp.bfloat16).astype(jnp.float32))
        value = value - terms[-1]
    return jnp.concatenate(terms, axis=0)


def synth_kernel(
    blks, bands, amps_hbm, beam_hbm, leg_hbm, order_hbm, cycle_hbm, count_hbm, noise_hbm,
    out_ref, order, cycle, count, noise, extra_ref,
    amps, beam, leg, weighted, wide, lists, sems,
):
    degrees = amps.shape[0]
    chunks = degrees // SLAB
    pairs = [(order_hbm, order), (cycle_hbm, cycle), (count_hbm, count), (beam_hbm, beam), (noise_hbm, noise)]
    for k in range(chunks):
        at = pl.ds(k * SLAB, SLAB)
        pairs.append((amps_hbm.at[at, :], amps.at[at, :]))
    pairs.append((leg_hbm, leg))
    copies = [pltpu.make_async_copy(src, dst, sems.at[n]) for n, (src, dst) in enumerate(pairs)]
    for copy in copies[3:4] + copies[5:] + copies[:3] + copies[4:5]:
        copy.start()
    copies[3].wait()
    lines = degrees // LANES
    rows = jnp.concatenate([beam[0:1, k * LANES : (k + 1) * LANES] for k in range(lines)], axis=0)
    wide[...] = spread(bf16_terms(rows), lines)
    extra_ref[...] = beam_rows(blks, bands, beam, lists)
    for k in range(chunks):
        copies[5 + k].wait()
        for j in range(k * SLAB, (k + 1) * SLAB, LANES):
            product = amps[j : j + LANES, :].astype(jnp.float32) * wide[:, j : j + LANES]
            weighted[j : j + LANES, :] = product.astype(jnp.bfloat16)
    for n in (0, 1, 2, 4, -1):
        copies[n].wait()
    total = jnp.dot(leg[...], weighted[...], preferred_element_type=jnp.float32)
    pair = 2 * total.shape[0] // blks
    for g, k in enumerate(member_order(blks)):
        out_ref[g * pair : (g + 1) * pair, :] = total[k // 2 * pair : (k // 2 + 1) * pair, :]


def mod_exact(value, modulus):
    quotient = (value.astype(jnp.float32) / modulus.astype(jnp.float32)).astype(jnp.int32)
    left = value - quotient * modulus
    left = jnp.where(left < 0, left + modulus, left)
    return jnp.where(left >= modulus, left - modulus, left)


def cos_sin(numer, count):
    countf = count.astype(jnp.float32)
    quarter = ((2 * numer + (count >> 1)).astype(jnp.float32) / countf).astype(jnp.int32)
    rest = (2 * numer - quarter * count).astype(jnp.float32)
    angle = rest * (jnp.float32(math.pi / 2) / countf)
    square = angle * angle
    sin = angle * (
        1.0 + square * (-1.0 / 6 + square * (1.0 / 120 + square * (-1.0 / 5040 + square * (1.0 / 362880))))
    )
    cos = 1.0 + square * (
        -0.5 + square * (1.0 / 24 + square * (-1.0 / 720 + square * (1.0 / 40320 - square * (1.0 / 3628800))))
    )
    odd = (quarter & 1) == 1
    cos_out = jnp.where(odd, sin, cos)
    sin_out = jnp.where(odd, cos, sin)
    cos_out = jnp.where(((quarter + 1) & 2) == 2, -cos_out, cos_out)
    sin_out = jnp.where((quarter & 2) == 2, -sin_out, sin_out)
    return cos_out, sin_out


def phase_tables(blks, pixels, cycles, order_ref, cycle_ref, count_ref):
    rows = blks * cycles
    start = lax.axis_index("blk") * cycles
    row = lax.broadcasted_iota(jnp.int32, (rows, LANES), 0)
    lane = lax.broadcasted_iota(jnp.int32, (rows, LANES), 1)
    slot = row % cycles
    count = jnp.zeros((rows, LANES), jnp.int32)
    parity = jnp.zeros((rows, LANES), jnp.int32)
    for i in range(cycles):
        cycle = cycle_ref[start + i]
        count = jnp.where(slot == i, count_ref[cycle], count)
        parity = jnp.where(slot == i, cycle & 1, parity)
    order = jnp.zeros((rows, LANES), jnp.int32)
    for g, k in enumerate(member_order(blks)):
        order = jnp.where(row // cycles == g, order_ref[k], order)
    fine_c, fine_s = cos_sin(mod_exact(2 * order * lane, 2 * count), count)
    coarse = 2 * LANES * order * (lane & (pixels // LANES - 1)) + order * parity
    coarse_c, coarse_s = cos_sin(mod_exact(coarse, 2 * count), count)
    norm = lax.rsqrt(count.astype(jnp.float32))
    return fine_c * norm, fine_s * norm, coarse_c, -coarse_s, count


def beam_rows(blks, bands, beam_ref, lists):
    blk = lax.axis_index("blk")
    part = beam_ref.shape[1] // bands
    lines = -(-part // LANES)
    lists[...] = jnp.zeros_like(lists)
    for p in range(bands):
        for t in range(lines):
            size = min(LANES, part - t * LANES)
            first = p * part + t * LANES
            value = beam_ref[0:1, first : first + size]
            for term in range(TERMS):
                top = value.astype(jnp.bfloat16).astype(jnp.float32)
                at = p * (blks // 2) * EXTRA + term * lines + t
                lists[at : at + 1, :size] = top
                value = value - top
    starts = [pl.multiple_of((p * (blks // 2) + blk // 2) * EXTRA, EXTRA) for p in range(bands)]
    return jnp.concatenate([lists[pl.ds(at, EXTRA), :] for at in starts], axis=0)


def gram_kernel(order_ref, cycle_ref, count_ref, noise_ref, keep_ref, give_ref, high, low, whole):
    blks, blk = lax.axis_size("blk"), lax.axis_index("blk")
    rows = keep_ref.shape[0]
    cycles = rows // blks
    pixels = noise_ref.shape[1]
    fine_c, fine_s, coarse_c, coarse_s, count = phase_tables(blks, pixels, cycles, order_ref, cycle_ref, count_ref)
    pixel = lax.broadcasted_iota(jnp.int32, noise_ref.shape, 1)
    root = jnp.sqrt(jnp.where(pixel < count[:cycles, :1], noise_ref[...], 0.0))
    root = jnp.concatenate([root] * max(8 // cycles, 1), axis=0)
    period = root.shape[0]
    step = 2
    total = jnp.zeros((2 * rows, 4 * rows), jnp.float32)
    for block in range(pixels // LANES // step):
        for j in range(block * step, (block + 1) * step):
            cols = slice(j * LANES, (j + 1) * LANES)
            here = jnp.concatenate([root[:, cols]] * (rows // period), axis=0)
            a_c, a_s = coarse_c[:, j : j + 1], coarse_s[:, j : j + 1]
            for c, value in enumerate((a_c * fine_c + a_s * fine_s, a_s * fine_c - a_c * fine_s)):
                value = value * here
                top = value.astype(jnp.bfloat16)
                rest = (value - top.astype(jnp.float32)).astype(jnp.bfloat16)
                for p in range(2):
                    to = slice(p * rows + c * (rows // 2), p * rows + (c + 1) * (rows // 2))
                    of = slice(p * (rows // 2), (p + 1) * (rows // 2))
                    high[to, cols] = top[of]
                    low[to, cols] = rest[of]
        cols = slice(block * step * LANES, (block + 1) * step * LANES)
        top = high[:, cols]
        both = jnp.concatenate([top, low[:, cols]], axis=0)
        total = total + lax.dot_general(top, both, NT, preferred_element_type=jnp.float32)
    cross = total[:, 2 * rows :]
    gram = total[:, : 2 * rows] + cross + cross.T
    row = lax.broadcasted_iota(jnp.int32, gram.shape, 0)
    col = lax.broadcasted_iota(jnp.int32, gram.shape, 1)
    gram = jnp.where(row % cycles == col % cycles, gram, 0.0)
    top = gram.astype(jnp.bfloat16)
    rest = (gram - top.astype(jnp.float32)).astype(jnp.bfloat16)
    whole[...] = jnp.concatenate([top, rest], axis=1)
    upper = (blk // 2 >= blks // 4).astype(jnp.int32)
    mine = pl.multiple_of((blk + upper) % 2 * rows, 16)
    keep_ref[...] = whole[pl.ds(mine, rows), :]
    give_ref[...] = whole[pl.ds(pl.multiple_of(rows - mine, 16), rows), :]


def apply_kernel(bands, keep_ref, got_ref, modes_ref, extra_ref, out_ref):
    rows = keep_ref.shape[0]
    terms = keep_ref.shape[1] // 2
    pair, width = EXTRA, modes_ref.shape[1]
    chains = width // 2
    first = lax.axis_index("blk") % 2 == 0
    keep, got = keep_ref[...], got_ref[...]
    modes = modes_ref[...].reshape(rows // pair, 2, pair, width)
    even, odd = modes[:, 0], modes[:, 1]
    near = lax.broadcasted_iota(jnp.int32, even.shape, 1) < pair // 2
    halves = []
    for e in range(2):
        if e == 0:
            x = jnp.where(near, even, pltpu.roll(odd, pair // 2, 1))
            matrix = jnp.where(first, keep, got)
        else:
            x = jnp.where(near, pltpu.roll(even, pair // 2, 1), odd)
            matrix = jnp.where(first, got, keep)
        x = x.reshape(rows, width)
        stacked = []
        for p in range(2):
            block = x[p * (rows // 2) : (p + 1) * (rows // 2)]
            stacked += [block[:, :chains], block[:, chains:]]
        stacked = jnp.concatenate(stacked, axis=0)
        top = stacked.astype(jnp.bfloat16)
        rest = (stacked - top.astype(jnp.float32)).astype(jnp.bfloat16)
        right = jnp.concatenate([top, rest, top], axis=0)
        matrix = jnp.concatenate([matrix[:, :terms], matrix], axis=1)
        result = jnp.dot(matrix, right, preferred_element_type=jnp.float32)
        half = jnp.concatenate([result[: rows // 2], result[rows // 2 :]], axis=1)
        halves.append(half.reshape(rows // 2 // pair, pair, width))
    near = near[: rows // 2 // pair]
    even = jnp.where(near, halves[0], pltpu.roll(halves[1], pair // 2, 1))
    odd = jnp.where(near, pltpu.roll(halves[0], pair // 2, 1), halves[1])
    size = pair + EXTRA
    for j in range(rows // pair):
        half = (even if j % 2 == 0 else odd)[j // 2]
        for b in range(bands):
            at = (j * bands + bands - 1 - b) * size
            piece = jnp.concatenate([half, extra_ref[b * EXTRA : (b + 1) * EXTRA, :]], axis=0)
            out_ref[at : at + size, :] = piece.astype(jnp.bfloat16)


def turn_kernel(leg_ref, out_ref):
    cycles, part = leg_ref.shape
    for t in range(0, part, LANES):
        size = min(LANES, part - t)
        out_ref[t : t + size, :] = leg_ref[:, t : t + size].astype(jnp.float32).T.astype(jnp.bfloat16)


def analysis_kernel(bands, leg_ref, half_ref, out_hbm, out, sems):
    part, cycles = leg_ref.shape
    width = half_ref.shape[1]
    lines = -(-part // LANES)
    size = 2 * EXTRA
    pairs = half_ref.shape[0] // size // bands
    got = half_ref[...].astype(jnp.float32).reshape(pairs, bands, size, width)
    place = [k // 2 for k in member_order(2 * pairs)[:pairs]]
    place = [place.index(p) for p in range(pairs)]
    right, columns = [], []
    for b in range(bands):
        mine = got[:, bands - 1 - b]
        right.append(jnp.concatenate([mine[place[p], :EXTRA] for p in range(pairs)], axis=0))
        used = -(-TERMS * lines // EXTRA)
        terms = jnp.concatenate([mine[place[p], EXTRA:] for p in range(used)], axis=0)
        gains = terms[:lines]
        for term in range(1, TERMS):
            gains = gains + terms[term * lines : (term + 1) * lines]
        columns.append(gains.T)
    right = jnp.concatenate(right, axis=1).astype(jnp.bfloat16)
    copies = []
    for k in range(len(out_sizes(part))):
        first, many = out_sizes(part)[k]
        product = jnp.dot(leg_ref[first : first + many, :], right, preferred_element_type=jnp.float32)
        for t in range(first, first + many, LANES):
            rows = slice(t, min(t + LANES, part))
            here = product[t - first : t - first + LANES]
            total = None
            for b in range(bands):
                add = columns[b][: here.shape[0], t // LANES : t // LANES + 1] * here[:, b * width : (b + 1) * width]
                total = add if total is None else total + add
            out[rows, :] = total
        at = pl.ds(first, many)
        copies.append(pltpu.make_async_copy(out.at[at, :], out_hbm.at[at, :], sems.at[k]))
        copies[-1].start()
    for copy in copies:
        copy.wait()


def out_sizes(part):
    step = 256
    return [(at, min(step, part - at)) for at in range(0, part, step)]


def shards(bands, amps, beam, legendre, m_values, cycle_order, pixel_counts, inv_noise):
    degrees, _, width = amps.shape
    cycles = legendre.shape[2]
    cycles_here = inv_noise.shape[1]
    orders = m_values.shape[0]
    rows = orders * cycles_here
    part = degrees // bands
    leg = jnp.swapaxes(legendre[0], 0, 1)
    smem = pl.BlockSpec(memory_space=pltpu.SMEM)
    vmem = pl.BlockSpec(memory_space=pltpu.VMEM)

    hbm = pl.BlockSpec(memory_space=pltpu.HBM)
    blks = lax.axis_size("blk")
    pair = 2 * cycles_here
    assert orders == blks and blks % 2 == 0 and pair == EXTRA and cycles == cycles_here * blks
    slabs = degrees // SLAB
    pixels = inv_noise.shape[2]
    sent, *gram_inputs, extra = pl.pallas_call(
        functools.partial(synth_kernel, blks, bands),
        out_shape=[
            jax.ShapeDtypeStruct((blks * pair, width), jnp.float32),
            pltpu.VMEM(m_values.shape, jnp.int32),
            pltpu.VMEM(cycle_order.shape, jnp.int32),
            pltpu.VMEM(pixel_counts.shape, jnp.int32),
            pltpu.VMEM((cycles_here, pixels), jnp.float32),
            pltpu.VMEM((bands * EXTRA, LANES), jnp.float32),
        ],
        in_specs=[hbm] * 7,
        out_specs=[vmem] * 6,
        scratch_shapes=[
            pltpu.VMEM((degrees, width), jnp.bfloat16),
            pltpu.VMEM((1, degrees), jnp.float32),
            pltpu.VMEM((cycles, degrees), jnp.bfloat16),
            pltpu.VMEM((degrees, width), jnp.bfloat16),
            pltpu.VMEM((LANES, degrees), jnp.float32),
            pltpu.VMEM((bands * (blks // 2) * EXTRA, LANES), jnp.float32),
            pltpu.SemaphoreType.DMA((6 + slabs,)),
        ],
        compiler_params=pltpu.CompilerParams(vmem_limit_bytes=62 * 1024 * 1024),
        cost_estimate=pl.CostEstimate(
            flops=2000 * degrees * cycles * width, transcendentals=0, bytes_accessed=0
        ),
    )(amps[:, 0, :], beam, leg, m_values, cycle_order, pixel_counts, inv_noise[0])
    modes = lax.all_to_all(
        sent, "blk", split_axis=0, concat_axis=0, tiled=True, axis_index_groups=[member_order(blks)]
    )

    keep, give = pl.pallas_call(
        gram_kernel,
        out_shape=[jax.ShapeDtypeStruct((rows, 4 * rows), jnp.bfloat16)] * 2,
        in_specs=[smem] * 3 + [vmem],
        out_specs=[vmem] * 2,
        scratch_shapes=[pltpu.VMEM((2 * rows, pixels), jnp.bfloat16)] * 2
        + [pltpu.VMEM((2 * rows, 4 * rows), jnp.bfloat16)],
        compiler_params=VMEM,
        cost_estimate=pl.CostEstimate(
            flops=16 * rows * rows * pixels, transcendentals=0, bytes_accessed=8 * rows * pixels
        ),
    )(*gram_inputs)
    got = lax.ppermute(give, "blk", [(k, k ^ 1) for k in range(blks)])

    leg_part = lax.dynamic_slice_in_dim(leg, lax.axis_index("band") * part, part, axis=1)
    leg_turned = pl.pallas_call(
        turn_kernel,
        out_shape=jax.ShapeDtypeStruct((part, cycles), jnp.bfloat16),
        in_specs=[vmem],
        out_specs=vmem,
        compiler_params=VMEM,
        cost_estimate=pl.CostEstimate(flops=part * cycles, transcendentals=0, bytes_accessed=4 * part * cycles),
    )(leg_part)
    size = pair + EXTRA
    half = pl.pallas_call(
        functools.partial(apply_kernel, bands),
        out_shape=jax.ShapeDtypeStruct((bands * (blks // 2) * size, width), jnp.bfloat16),
        in_specs=[vmem] * 4,
        out_specs=vmem,
        compiler_params=VMEM,
    )(keep, got, modes, extra)
    half, leg_turned = lax.optimization_barrier((half, leg_turned))
    order = member_order(blks)
    groups = [
        [b * blks + k for k in members for b in reversed(range(bands))]
        for members in (order[: blks // 2], order[blks // 2 :])
    ]
    half = lax.all_to_all(
        half, ("band", "blk"), split_axis=0, concat_axis=0, tiled=True, axis_index_groups=groups
    )

    out = pl.pallas_call(
        functools.partial(analysis_kernel, bands),
        out_shape=jax.ShapeDtypeStruct((part, width), jnp.float32),
        in_specs=[vmem] * 2,
        out_specs=hbm,
        scratch_shapes=[
            pltpu.VMEM((part, width), jnp.float32),
            pltpu.SemaphoreType.DMA((len(out_sizes(part)),)),
        ],
        compiler_params=VMEM,
    )(leg_turned, half)
    return out[:, None, :]


def solution(mesh):
    return jax.shard_map(
        functools.partial(shards, mesh.shape["band"]),
        mesh=mesh,
        in_specs=(
            P(None, "blk", None),
            P("band", None),
            P("blk", None, None),
            P(),
            P(),
            P(),
            P("band", "blk", None),
        ),
        out_specs=P("band", "blk", None),
        check_vma=False,
    )
```

```python
import functools
import math

import jax
import jax.numpy as jnp
from jax import lax
from jax.experimental import pallas as pl
from jax.experimental.pallas import tpu as pltpu
from jax.sharding import PartitionSpec as P

LANES = 128
SLAB = 1280
EXTRA = 8
TERMS = 3
VMEM = pltpu.CompilerParams(vmem_limit_bytes=48 * 1024 * 1024)
NT = (((1,), (1,)), ((), ()))


def member_order(blks):
    pairs = blks // 2
    quarter = pairs // 4
    order = [q * quarter + i for q in (2, 3, 1, 0) for i in reversed(range(quarter))]
    upper = [int(p >= pairs // 2) for p in range(pairs)]
    return [2 * p + upper[p] for p in order] + [2 * p + 1 - upper[p] for p in order]


def spread(rows, lines):
    count = rows.shape[0]
    term = lax.broadcasted_iota(jnp.int32, (count, lines * LANES), 0) % lines
    block = lax.broadcasted_iota(jnp.int32, (count, lines * LANES), 1) // LANES
    pick = jnp.where(term == block, 1.0, 0.0).astype(jnp.bfloat16)
    return jnp.dot(rows.T.astype(jnp.bfloat16), pick, preferred_element_type=jnp.float32)


def bf16_terms(value):
    terms = []
    for _ in range(TERMS):
        terms.append(value.astype(jnp.bfloat16).astype(jnp.float32))
        value = value - terms[-1]
    return jnp.concatenate(terms, axis=0)


def synth_kernel(
    blks, bands, amps_hbm, beam_hbm, leg_hbm, order_hbm, cycle_hbm, count_hbm, noise_hbm,
    out_ref, order, cycle, count, noise, extra_ref,
    amps, beam, leg, weighted, wide, lists, sems,
):
    degrees = amps.shape[0]
    chunks = degrees // SLAB
    pairs = [(order_hbm, order), (cycle_hbm, cycle), (count_hbm, count), (beam_hbm, beam), (noise_hbm, noise)]
    for k in range(chunks):
        at = pl.ds(k * SLAB, SLAB)
        pairs.append((amps_hbm.at[at, :], amps.at[at, :]))
    half = leg.shape[0] // 2
    for k in range(2):
        pairs.append((leg_hbm.at[pl.ds(k * half, half), :], leg.at[pl.ds(k * half, half), :]))
    copies = [pltpu.make_async_copy(src, dst, sems.at[n]) for n, (src, dst) in enumerate(pairs)]
    for copy in copies[3:4] + copies[5:] + copies[:3] + copies[4:5]:
        copy.start()
    copies[3].wait()
    lines = degrees // LANES
    rows = jnp.concatenate([beam[0:1, k * LANES : (k + 1) * LANES] for k in range(lines)], axis=0)
    wide[...] = spread(bf16_terms(rows), lines)
    extra_ref[...] = beam_rows(blks, bands, beam, lists)
    for k in range(chunks):
        copies[5 + k].wait()
        for j in range(k * SLAB, (k + 1) * SLAB, LANES):
            product = amps[j : j + LANES, :].astype(jnp.float32) * wide[:, j : j + LANES]
            weighted[j : j + LANES, :] = product.astype(jnp.bfloat16)
    for n in (0, 1, 2, 4, -2, -1):
        copies[n].wait()
    total = jnp.dot(leg[...], weighted[...], preferred_element_type=jnp.float32)
    pair = 2 * total.shape[0] // blks
    for g, k in enumerate(member_order(blks)):
        out_ref[g * pair : (g + 1) * pair, :] = total[k // 2 * pair : (k // 2 + 1) * pair, :]


def mod_exact(value, modulus):
    quotient = (value.astype(jnp.float32) / modulus.astype(jnp.float32)).astype(jnp.int32)
    left = value - quotient * modulus
    left = jnp.where(left < 0, left + modulus, left)
    return jnp.where(left >= modulus, left - modulus, left)


def cos_sin(numer, count):
    countf = count.astype(jnp.float32)
    quarter = ((2 * numer + (count >> 1)).astype(jnp.float32) / countf).astype(jnp.int32)
    rest = (2 * numer - quarter * count).astype(jnp.float32)
    angle = rest * (jnp.float32(math.pi / 2) / countf)
    square = angle * angle
    sin = angle * (
        1.0 + square * (-1.0 / 6 + square * (1.0 / 120 + square * (-1.0 / 5040 + square * (1.0 / 362880))))
    )
    cos = 1.0 + square * (
        -0.5 + square * (1.0 / 24 + square * (-1.0 / 720 + square * (1.0 / 40320 - square * (1.0 / 3628800))))
    )
    odd = (quarter & 1) == 1
    cos_out = jnp.where(odd, sin, cos)
    sin_out = jnp.where(odd, cos, sin)
    cos_out = jnp.where(((quarter + 1) & 2) == 2, -cos_out, cos_out)
    sin_out = jnp.where((quarter & 2) == 2, -sin_out, sin_out)
    return cos_out, sin_out


def phase_tables(blks, pixels, cycles, order_ref, cycle_ref, count_ref):
    rows = blks * cycles
    start = lax.axis_index("blk") * cycles
    row = lax.broadcasted_iota(jnp.int32, (rows, LANES), 0)
    lane = lax.broadcasted_iota(jnp.int32, (rows, LANES), 1)
    slot = row % cycles
    count = jnp.zeros((rows, LANES), jnp.int32)
    parity = jnp.zeros((rows, LANES), jnp.int32)
    for i in range(cycles):
        cycle = cycle_ref[start + i]
        count = jnp.where(slot == i, count_ref[cycle], count)
        parity = jnp.where(slot == i, cycle & 1, parity)
    order = jnp.zeros((rows, LANES), jnp.int32)
    for g, k in enumerate(member_order(blks)):
        order = jnp.where(row // cycles == g, order_ref[k], order)
    fine_c, fine_s = cos_sin(mod_exact(2 * order * lane, 2 * count), count)
    coarse = 2 * LANES * order * (lane & (pixels // LANES - 1)) + order * parity
    coarse_c, coarse_s = cos_sin(mod_exact(coarse, 2 * count), count)
    norm = lax.rsqrt(count.astype(jnp.float32))
    return fine_c * norm, fine_s * norm, coarse_c, -coarse_s, count


def beam_rows(blks, bands, beam_ref, lists):
    blk = lax.axis_index("blk")
    part = beam_ref.shape[1] // bands
    lines = -(-part // LANES)
    lists[...] = jnp.zeros_like(lists)
    for p in range(bands):
        for t in range(lines):
            size = min(LANES, part - t * LANES)
            first = p * part + t * LANES
            value = beam_ref[0:1, first : first + size]
            for term in range(TERMS):
                top = value.astype(jnp.bfloat16).astype(jnp.float32)
                at = p * (blks // 2) * EXTRA + term * lines + t
                lists[at : at + 1, :size] = top
                value = value - top
    starts = [pl.multiple_of((p * (blks // 2) + blk // 2) * EXTRA, EXTRA) for p in range(bands)]
    return jnp.concatenate([lists[pl.ds(at, EXTRA), :] for at in starts], axis=0)


def gram_kernel(order_ref, cycle_ref, count_ref, noise_ref, keep_ref, give_ref, high, low, whole):
    blks, blk = lax.axis_size("blk"), lax.axis_index("blk")
    rows = keep_ref.shape[0]
    cycles = rows // blks
    pixels = noise_ref.shape[1]
    fine_c, fine_s, coarse_c, coarse_s, count = phase_tables(blks, pixels, cycles, order_ref, cycle_ref, count_ref)
    pixel = lax.broadcasted_iota(jnp.int32, noise_ref.shape, 1)
    root = jnp.sqrt(jnp.where(pixel < count[:cycles, :1], noise_ref[...], 0.0))
    root = jnp.concatenate([root] * max(8 // cycles, 1), axis=0)
    period = root.shape[0]
    step = 2
    total = jnp.zeros((2 * rows, 4 * rows), jnp.float32)
    for block in range(pixels // LANES // step):
        for j in range(block * step, (block + 1) * step):
            cols = slice(j * LANES, (j + 1) * LANES)
            here = jnp.concatenate([root[:, cols]] * (rows // period), axis=0)
            a_c, a_s = coarse_c[:, j : j + 1], coarse_s[:, j : j + 1]
            for c, value in enumerate((a_c * fine_c + a_s * fine_s, a_s * fine_c - a_c * fine_s)):
                value = value * here
                top = value.astype(jnp.bfloat16)
                rest = (value - top.astype(jnp.float32)).astype(jnp.bfloat16)
                for p in range(2):
                    to = slice(p * rows + c * (rows // 2), p * rows + (c + 1) * (rows // 2))
                    of = slice(p * (rows // 2), (p + 1) * (rows // 2))
                    high[to, cols] = top[of]
                    low[to, cols] = rest[of]
        cols = slice(block * step * LANES, (block + 1) * step * LANES)
        top = high[:, cols]
        both = jnp.concatenate([top, low[:, cols]], axis=0)
        total = total + lax.dot_general(top, both, NT, preferred_element_type=jnp.float32)
    cross = total[:, 2 * rows :]
    gram = total[:, : 2 * rows] + cross + cross.T
    row = lax.broadcasted_iota(jnp.int32, gram.shape, 0)
    col = lax.broadcasted_iota(jnp.int32, gram.shape, 1)
    gram = jnp.where(row % cycles == col % cycles, gram, 0.0)
    top = gram.astype(jnp.bfloat16)
    rest = (gram - top.astype(jnp.float32)).astype(jnp.bfloat16)
    whole[...] = jnp.concatenate([top, rest], axis=1)
    upper = (blk // 2 >= blks // 4).astype(jnp.int32)
    mine = pl.multiple_of((blk + upper) % 2 * rows, 16)
    keep_ref[...] = whole[pl.ds(mine, rows), :]
    give_ref[...] = whole[pl.ds(pl.multiple_of(rows - mine, 16), rows), :]


def apply_kernel(bands, keep_ref, got_ref, modes_ref, extra_ref, out_ref):
    rows = keep_ref.shape[0]
    terms = keep_ref.shape[1] // 2
    pair, width = EXTRA, modes_ref.shape[1]
    chains = width // 2
    first = lax.axis_index("blk") % 2 == 0
    keep, got = keep_ref[...], got_ref[...]
    modes = modes_ref[...].reshape(rows // pair, 2, pair, width)
    even, odd = modes[:, 0], modes[:, 1]
    near = lax.broadcasted_iota(jnp.int32, even.shape, 1) < pair // 2
    halves = []
    for e in range(2):
        if e == 0:
            x = jnp.where(near, even, pltpu.roll(odd, pair // 2, 1))
            matrix = jnp.where(first, keep, got)
        else:
            x = jnp.where(near, pltpu.roll(even, pair // 2, 1), odd)
            matrix = jnp.where(first, got, keep)
        x = x.reshape(rows, width)
        stacked = []
        for p in range(2):
            block = x[p * (rows // 2) : (p + 1) * (rows // 2)]
            stacked += [block[:, :chains], block[:, chains:]]
        stacked = jnp.concatenate(stacked, axis=0)
        top = stacked.astype(jnp.bfloat16)
        rest = (stacked - top.astype(jnp.float32)).astype(jnp.bfloat16)
        right = jnp.concatenate([top, rest, top], axis=0)
        matrix = jnp.concatenate([matrix[:, :terms], matrix], axis=1)
        result = jnp.dot(matrix, right, preferred_element_type=jnp.float32)
        half = jnp.concatenate([result[: rows // 2], result[rows // 2 :]], axis=1)
        halves.append(half.reshape(rows // 2 // pair, pair, width))
    near = near[: rows // 2 // pair]
    even = jnp.where(near, halves[0], pltpu.roll(halves[1], pair // 2, 1))
    odd = jnp.where(near, pltpu.roll(halves[0], pair // 2, 1), halves[1])
    size = pair + EXTRA
    for j in range(rows // pair):
        half = (even if j % 2 == 0 else odd)[j // 2]
        for b in range(bands):
            at = (j * bands + bands - 1 - b) * size
            piece = jnp.concatenate([half, extra_ref[b * EXTRA : (b + 1) * EXTRA, :]], axis=0)
            out_ref[at : at + size, :] = piece.astype(jnp.bfloat16)


def turn_kernel(leg_ref, out_ref):
    cycles, part = leg_ref.shape
    for t in range(0, part, LANES):
        size = min(LANES, part - t)
        out_ref[t : t + size, :] = leg_ref[:, t : t + size].astype(jnp.float32).T.astype(jnp.bfloat16)


def analysis_kernel(bands, leg_ref, half_ref, out_hbm, out, sems):
    part, cycles = leg_ref.shape
    width = half_ref.shape[1]
    lines = -(-part // LANES)
    size = 2 * EXTRA
    pairs = half_ref.shape[0] // size // bands
    got = half_ref[...].astype(jnp.float32).reshape(pairs, bands, size, width)
    place = [k // 2 for k in member_order(2 * pairs)[:pairs]]
    place = [place.index(p) for p in range(pairs)]
    right, columns = [], []
    for b in range(bands):
        mine = got[:, bands - 1 - b]
        right.append(jnp.concatenate([mine[place[p], :EXTRA] for p in range(pairs)], axis=0))
        used = -(-TERMS * lines // EXTRA)
        terms = jnp.concatenate([mine[place[p], EXTRA:] for p in range(used)], axis=0)
        gains = terms[:lines]
        for term in range(1, TERMS):
            gains = gains + terms[term * lines : (term + 1) * lines]
        columns.append(gains.T)
    right = jnp.concatenate(right, axis=1).astype(jnp.bfloat16)
    copies = []
    for k in range(len(out_sizes(part))):
        first, many = out_sizes(part)[k]
        product = jnp.dot(leg_ref[first : first + many, :], right, preferred_element_type=jnp.float32)
        for t in range(first, first + many, LANES):
            rows = slice(t, min(t + LANES, part))
            here = product[t - first : t - first + LANES]
            total = None
            for b in range(bands):
                add = columns[b][: here.shape[0], t // LANES : t // LANES + 1] * here[:, b * width : (b + 1) * width]
                total = add if total is None else total + add
            out[rows, :] = total
        at = pl.ds(first, many)
        copies.append(pltpu.make_async_copy(out.at[at, :], out_hbm.at[at, :], sems.at[k]))
        copies[-1].start()
    for copy in copies:
        copy.wait()


def out_sizes(part):
    step = 256
    return [(at, min(step, part - at)) for at in range(0, part, step)]


def shards(bands, amps, beam, legendre, m_values, cycle_order, pixel_counts, inv_noise):
    degrees, _, width = amps.shape
    cycles = legendre.shape[2]
    cycles_here = inv_noise.shape[1]
    orders = m_values.shape[0]
    rows = orders * cycles_here
    part = degrees // bands
    leg = jnp.swapaxes(legendre[0], 0, 1)
    smem = pl.BlockSpec(memory_space=pltpu.SMEM)
    vmem = pl.BlockSpec(memory_space=pltpu.VMEM)

    hbm = pl.BlockSpec(memory_space=pltpu.HBM)
    blks = lax.axis_size("blk")
    pair = 2 * cycles_here
    assert orders == blks and blks % 2 == 0 and pair == EXTRA and cycles == cycles_here * blks
    slabs = degrees // SLAB
    pixels = inv_noise.shape[2]
    sent, *gram_inputs, extra = pl.pallas_call(
        functools.partial(synth_kernel, blks, bands),
        out_shape=[
            jax.ShapeDtypeStruct((blks * pair, width), jnp.float32),
            pltpu.VMEM(m_values.shape, jnp.int32),
            pltpu.VMEM(cycle_order.shape, jnp.int32),
            pltpu.VMEM(pixel_counts.shape, jnp.int32),
            pltpu.VMEM((cycles_here, pixels), jnp.float32),
            pltpu.VMEM((bands * EXTRA, LANES), jnp.float32),
        ],
        in_specs=[hbm] * 7,
        out_specs=[vmem] * 6,
        scratch_shapes=[
            pltpu.VMEM((degrees, width), jnp.bfloat16),
            pltpu.VMEM((1, degrees), jnp.float32),
            pltpu.VMEM((cycles, degrees), jnp.bfloat16),
            pltpu.VMEM((degrees, width), jnp.bfloat16),
            pltpu.VMEM((LANES, degrees), jnp.float32),
            pltpu.VMEM((bands * (blks // 2) * EXTRA, LANES), jnp.float32),
            pltpu.SemaphoreType.DMA((7 + slabs,)),
        ],
        compiler_params=pltpu.CompilerParams(vmem_limit_bytes=62 * 1024 * 1024),
        cost_estimate=pl.CostEstimate(
            flops=2000 * degrees * cycles * width, transcendentals=0, bytes_accessed=0
        ),
    )(amps[:, 0, :], beam, leg, m_values, cycle_order, pixel_counts, inv_noise[0])
    modes = lax.all_to_all(
        sent, "blk", split_axis=0, concat_axis=0, tiled=True, axis_index_groups=[member_order(blks)]
    )

    keep, give = pl.pallas_call(
        gram_kernel,
        out_shape=[jax.ShapeDtypeStruct((rows, 4 * rows), jnp.bfloat16)] * 2,
        in_specs=[smem] * 3 + [vmem],
        out_specs=[vmem] * 2,
        scratch_shapes=[pltpu.VMEM((2 * rows, pixels), jnp.bfloat16)] * 2
        + [pltpu.VMEM((2 * rows, 4 * rows), jnp.bfloat16)],
        compiler_params=VMEM,
        cost_estimate=pl.CostEstimate(
            flops=16 * rows * rows * pixels, transcendentals=0, bytes_accessed=8 * rows * pixels
        ),
    )(*gram_inputs)
    got = lax.ppermute(give, "blk", [(k, k ^ 1) for k in range(blks)])

    leg_part = lax.dynamic_slice_in_dim(leg, lax.axis_index("band") * part, part, axis=1)
    leg_turned = pl.pallas_call(
        turn_kernel,
        out_shape=jax.ShapeDtypeStruct((part, cycles), jnp.bfloat16),
        in_specs=[vmem],
        out_specs=vmem,
        compiler_params=VMEM,
        cost_estimate=pl.CostEstimate(flops=part * cycles, transcendentals=0, bytes_accessed=4 * part * cycles),
    )(leg_part)
    size = pair + EXTRA
    half = pl.pallas_call(
        functools.partial(apply_kernel, bands),
        out_shape=jax.ShapeDtypeStruct((bands * (blks // 2) * size, width), jnp.bfloat16),
        in_specs=[vmem] * 4,
        out_specs=vmem,
        compiler_params=VMEM,
    )(keep, got, modes, extra)
    half, leg_turned = lax.optimization_barrier((half, leg_turned))
    order = member_order(blks)
    groups = [
        [b * blks + k for k in members for b in reversed(range(bands))]
        for members in (order[: blks // 2], order[blks // 2 :])
    ]
    half = lax.all_to_all(
        half, ("band", "blk"), split_axis=0, concat_axis=0, tiled=True, axis_index_groups=groups
    )

    out = pl.pallas_call(
        functools.partial(analysis_kernel, bands),
        out_shape=jax.ShapeDtypeStruct((part, width), jnp.float32),
        in_specs=[vmem] * 2,
        out_specs=hbm,
        scratch_shapes=[
            pltpu.VMEM((part, width), jnp.float32),
            pltpu.SemaphoreType.DMA((len(out_sizes(part)),)),
        ],
        compiler_params=VMEM,
    )(leg_turned, half)
    return out[:, None, :]


def solution(mesh):
    return jax.shard_map(
        functools.partial(shards, mesh.shape["band"]),
        mesh=mesh,
        in_specs=(
            P(None, "blk", None),
            P("band", None),
            P("blk", None, None),
            P(),
            P(),
            P(),
            P("band", "blk", None),
        ),
        out_specs=P("band", "blk", None),
        check_vma=False,
    )
```
